1024 devices in a mesh: row: 4 (over y_lo, core), col: 16 (over y_hi, x), depth: 16 (over z).
Axes of the slice: x: 4, y: 8 (y_hi: 4, y_lo: 2; y = y_hi * 2 + y_lo), z: 16, core: 2. Of those that a mesh axis runs over, the one named last changes fastest.
Arguments:
- inputs: bfloat16 [3072, 12288], P(('row', 'col'), 'depth'), may hold values from -0.107910156 to 0.107910156
- weight: bfloat16 [12288, 18432], P('depth', 'col'), may hold values from -0.0546875 to 0.0546875
- grad_out: bfloat16 [3072, 18432], P(('row', 'depth'), 'col'), may hold values from -16 to 16
Outputs:
- grad_inputs: bfloat16 [3072, 12288], P(('row', 'col'), 'depth')
- grad_weight: bfloat16 [12288, 18432], P(('depth', 'row'), 'col')
The draws below stay inside these ranges and needn't reach their ends.
All inputs are finite; a program needn't handle non-finite values.
Results may differ from the reference program's by a relative error of at most 0.001.
Values may be sent and summed in bfloat16 or wider, within the bound.
No kernel may reach another device: no remote copies, remote signals or barrier semaphores. Data moves between devices by JAX's collectives and lax.ppermute only.
A program may use at most 32 MiB of HBM per device.

```python
import jax
import jax.numpy as jnp
from jax import lax

D = 12288
FW = 18432
TOKENS = 3072


def with_spikes(values, own_key, source, target, parts, factor):
    owner, partner = [(jnp.arange(values.shape[position]) // (values.shape[position] // parts)).reshape([-1 if axis == position else 1 for axis in range(values.ndim)]) for position in (source, target)]
    chosen = jax.random.permutation(own_key, parts)[partner]
    strong = (owner == chosen) | (owner == (partner + parts // 2) % parts)
    return jnp.where(strong, factor * values, values)


def block_levels(key, dims, pieces, smallest, high):
    def one(dim, blocks):
        draws = jax.random.uniform(jax.random.fold_in(jax.random.fold_in(key, 6), dim), (blocks,), jnp.float32, smallest / len(pieces), high / len(pieces))
        return jnp.repeat(jnp.exp(draws), dims[dim] // blocks).reshape((-1,) + (1,) * (len(dims) - dim - 1))

    factor_of = one(*pieces[0])
    for cut in pieces[1:]:
        factor_of = factor_of * one(*cut)
    return factor_of


def normal_values(rng, extent, scale, reach, pieces=(), held_as=jnp.bfloat16):
    gain = block_levels(rng, extent, pieces, -0.22, 0.18) if pieces else 1.0
    entries = jax.random.normal(rng, extent, jnp.float32) * scale * gain
    return jnp.minimum(jnp.maximum(entries, -reach), reach).astype(held_as)


def gaussian_with(stream_key, dims, spread, reach, shards, heavy, dtype=jnp.bfloat16):
    values = spread * jax.random.normal(stream_key, dims, jnp.float32)
    if shards:
        values = values * block_levels(stream_key, dims, shards, -0.22, 0.18)
    return jnp.clip(with_spikes(values, jax.random.fold_in(stream_key, 3), *heavy), -reach, reach).astype(dtype)


def setup_inputs(seed: int = 0) -> dict:
    arg_keys = jax.random.split(jax.random.key(seed), 4)
    return {
        "inputs": normal_values(arg_keys[0], (TOKENS, D), (TOKENS ** -0.5), 0.107910156, ((0, 64), (1, 16))),
        "weight": normal_values(arg_keys[1], (D, FW), D ** -0.5, 0.0546875, ((0, 16), (1, 16))),
        "grad_out": gaussian_with(arg_keys[2], (TOKENS, FW), 1.0, 16.0, ((0, 64), (1, 16)), (1, 0, 64, 4.0)),
    }


def reference(inputs, weight, grad_out):
    grad_inputs = lax.dot_general(grad_out, weight, (((1,), (1,)), ((), ())), preferred_element_type=jnp.float32)
    grad_weight = lax.dot_general(inputs, grad_out, (((0,), (0,)), ((), ())), preferred_element_type=jnp.float32)
    return grad_inputs.astype(jnp.bfloat16), grad_weight.astype(jnp.bfloat16)
```

```python
import functools

import jax
import jax.numpy as jnp
from jax import lax
from jax.experimental import pallas as pl
from jax.experimental.pallas import tpu as pltpu
from jax.sharding import PartitionSpec as P

F32 = jnp.float32
BF16 = jnp.bfloat16
VMEM = pl.BlockSpec(memory_space=pltpu.VMEM)
SMEM = pl.BlockSpec(memory_space=pltpu.SMEM)
ORDER = (0, 1, 3, 2)


def swap_x(value, j):
    return lax.ppermute(value, "col", [(i, i ^ j) for i in range(16)])


def swap_y(value, j):
    return lax.ppermute(value, "col", [(i, i ^ (4 * j)) for i in range(16)])


def swap_row(value, j):
    return lax.ppermute(value, "row", [(i, i ^ j) for i in range(4)])


def place(where, piece):
    return jnp.bitwise_xor(where, piece)


def grad_inputs_kernel(col_ref, grad_ref, weight_ref, send_a, send_b, keep_a, keep_b, rows):
    block = grad_ref.shape[0] // 16
    half = weight_ref.shape[0] // 2
    me = col_ref[0]
    for jx in range(4):
        for jy in range(4):
            source = pl.multiple_of(place(me, jy * 4 + jx) * block, block)
            rows[pl.ds((jx * 4 + jy) * block, block), :] = grad_ref[pl.ds(source, block), :]
    quarter = 4 * block
    for out_half, (sent, kept, sends, keeps) in enumerate(
        ((send_a, keep_a, (1, 2), (0, 3)), (send_b, keep_b, (3, 2), (0, 1)))
    ):
        part = lax.dot_general(
            rows[...],
            weight_ref[pl.ds(out_half * half, half), :],
            (((1,), (1,)), ((), ())),
            preferred_element_type=F32,
        )
        for slot, jx in enumerate(sends):
            sent[pl.ds(slot * quarter, quarter), :] = part[jx * quarter : (jx + 1) * quarter]
        for slot, jx in enumerate(keeps):
            kept[pl.ds(slot * quarter, quarter), :] = part[jx * quarter : (jx + 1) * quarter]


def grad_weight_kernel(place_ref, grad_ref, own, y1, y3, x1, x3, sent, kept, tokens, total):
    block = own.shape[0]
    me, row = place_ref[0], place_ref[1]
    lead = 0
    for ref in (own, y1, y3, x1, x3):
        for k in range(ref.shape[0] // block):
            j = ORDER[(lead + k) % 4] * 4 + ORDER[(lead + k) // 4]
            target = pl.multiple_of(place(me, j) * block, block)
            tokens[pl.ds(target, block), :] = ref[pl.ds(k * block, block), :]
        lead += ref.shape[0] // block
    total[...] = lax.dot_general(
        tokens[...], grad_ref[...], (((0,), (0,)), ((), ())), preferred_element_type=F32
    )
    rows = total.shape[0] // 4
    for jy in range(2):
        for jc, ref in ((1, sent), (0, kept)):
            source = pl.multiple_of(place(row, jy * 2 + jc) * rows, rows)
            ref[pl.ds(jy * rows, rows), :] = total[pl.ds(source, rows), :]


def per_device(inputs, weight, grad_out):
    block, width = inputs.shape
    columns = weight.shape[1]
    col, row = lax.axis_index("col"), lax.axis_index("row")
    grad_rows = lax.all_gather(grad_out, "depth", axis=0, tiled=True)

    y1 = swap_y(inputs, 1)
    y3 = swap_y(jnp.concatenate([inputs, y1]), 3)
    x1 = swap_x(jnp.concatenate([inputs, y1, y3]), 1)
    x3 = swap_x(jnp.concatenate([inputs, y1, y3, x1]), 3)

    tokens = block * 16
    piece = jax.ShapeDtypeStruct((tokens // 2, width // 2), F32)
    send_a, send_b, keep_a, keep_b = pl.pallas_call(
        grad_inputs_kernel,
        out_shape=[piece] * 4,
        in_specs=[SMEM, VMEM, VMEM],
        out_specs=[VMEM] * 4,
        scratch_shapes=[pltpu.VMEM((tokens, columns), BF16)],
        compiler_params=pltpu.CompilerParams(vmem_limit_bytes=32 << 20),
        cost_estimate=pl.CostEstimate(
            flops=2 * tokens * width * columns, bytes_accessed=6 << 20, transcendentals=0
        ),
        name="grad_inputs",
    )(col.reshape(1), grad_rows, weight)
    got_a, got_b = swap_x(send_a, 1), swap_x(send_b, 3)

    half = jax.ShapeDtypeStruct((width // 2, columns), F32)
    send_w, keep_w = pl.pallas_call(
        grad_weight_kernel,
        out_shape=[half] * 2,
        in_specs=[SMEM] + [VMEM] * 6,
        out_specs=[VMEM] * 2,
        scratch_shapes=[pltpu.VMEM((tokens, width), BF16), pltpu.VMEM((width, columns), F32)],
        compiler_params=pltpu.CompilerParams(vmem_limit_bytes=32 << 20),
        cost_estimate=pl.CostEstimate(
            flops=2 * tokens * width * columns, bytes_accessed=7 << 20, transcendentals=0
        ),
        name="grad_weight",
    )(jnp.stack([col, row]), grad_rows, inputs, y1, y3, x1, x3)
    got_w = swap_row(send_w, 1)

    quarter = tokens // 4
    sum_a, sum_b = keep_a + got_a, keep_b + got_b
    got_a, got_b = swap_x(sum_a[quarter:], 3), swap_x(sum_b[quarter:], 1)

    rows = width // 4
    sum_w = keep_w + got_w
    got_w = swap_row(sum_w[rows:], 2)

    mine = jnp.concatenate([sum_a[:quarter] + got_a, sum_b[:quarter] + got_b], axis=1)
    mine = mine.reshape(4, block, width)
    grad_inputs = mine[0] + swap_y(mine[1], 1) + swap_y(mine[2], 2) + swap_y(mine[3], 3)
    grad_weight = sum_w[:rows] + got_w
    return grad_inputs.astype(BF16), grad_weight.astype(BF16)


def solution(mesh):
    placed = (P(("row", "col"), "depth"), P("depth", "col"), P(("row", "depth"), "col"))
    return jax.shard_map(
        per_device,
        mesh=mesh,
        in_specs=placed,
        out_specs=(P(("row", "col"), "depth"), P(("depth", "row"), "col")),
        check_vma=False,
    )
```

```python
import jax
import jax.numpy as jnp
from jax import lax
from jax.experimental import pallas as pl
from jax.experimental.pallas import tpu as pltpu
from jax.sharding import PartitionSpec as P

F32 = jnp.float32
BF16 = jnp.bfloat16
VMEM = pl.BlockSpec(memory_space=pltpu.VMEM)
SMEM = pl.BlockSpec(memory_space=pltpu.SMEM)
ORDER = (0, 1, 3, 2)


def swap_x(value, j):
    return lax.ppermute(value, "col", [(i, i ^ j) for i in range(16)])


def swap_y(value, j):
    return lax.ppermute(value, "col", [(i, i ^ (4 * j)) for i in range(16)])


def swap_row(value, j):
    return lax.ppermute(value, "row", [(i, i ^ j) for i in range(4)])


def shift_depth(value, k):
    return lax.ppermute(value, "depth", [(i, (i + k) % 16) for i in range(16)])


def grad_inputs_kernel(place_ref, *refs):
    chunks, (weight_ref, send_a, send_b, keep_a, keep_b, rows) = refs[:16], refs[16:]
    block = chunks[0].shape[0]
    half = weight_ref.shape[0] // 2
    depth, col = place_ref[0], place_ref[1]
    for k in range(16):
        j = jnp.bitwise_xor(jnp.bitwise_and(depth + k, 15), col)
        at = jnp.bitwise_xor(j, jnp.bitwise_and(jnp.right_shift(j, 1), 5))
        at = jnp.bitwise_and(at, 3) * 4 + jnp.right_shift(at, 2)
        rows[pl.ds(pl.multiple_of(at * block, block), block), :] = chunks[k][...]
    quarter = 4 * block
    for out_half, (sent, kept, sends, keeps) in enumerate(
        ((send_a, keep_a, (1, 2), (0, 3)), (send_b, keep_b, (3, 2), (0, 1)))
    ):
        part = lax.dot_general(
            rows[...],
            weight_ref[pl.ds(out_half * half, half), :],
            (((1,), (1,)), ((), ())),
            preferred_element_type=F32,
        )
        for ref, order in ((sent, sends), (kept, keeps)):
            for slot, jx in enumerate(order):
                at = ORDER.index(jx) * quarter
                ref[pl.ds(slot * quarter, quarter), :] = part[at : at + quarter]


def grad_weight_kernel(row_ref, rows_ref, own, y1, y3, x1, x3, sent, kept, tokens, total):
    at = 0
    for ref in (own, y1, y3, x1, x3):
        tokens[pl.ds(at, ref.shape[0]), :] = ref[...]
        at += ref.shape[0]
    total[...] = lax.dot_general(
        tokens[...], rows_ref[...], (((0,), (0,)), ((), ())), preferred_element_type=F32
    )
    rows = total.shape[0] // 4
    for jy in range(2):
        for jc, ref in ((1, sent), (0, kept)):
            source = jnp.bitwise_xor(row_ref[0], jy * 2 + jc) * rows
            ref[pl.ds(jy * rows, rows), :] = total[pl.ds(pl.multiple_of(source, rows), rows), :]


def after(*values):
    return lax.optimization_barrier(values)


def per_device(inputs, weight, grad_out):
    block, width = inputs.shape
    columns = weight.shape[1]
    tokens = block * 16
    depth, col, row = (lax.axis_index(a) for a in ("depth", "col", "row"))

    chunks = [grad_out] + [None] * 15
    held, parts = inputs, [inputs]
    for k in range(1, 9):
        up, down = chunks[(17 - k) % 16], chunks[k - 1]
        if k > 2:
            up, chunks[k - 2] = after(up, chunks[k - 2])
        chunks[16 - k] = shift_depth(up, 1)
        if k < 8:
            if k > 1:
                down, chunks[17 - k] = after(down, chunks[17 - k])
            chunks[k] = shift_depth(down, -1)
        swap = {1: (swap_y, 1), 3: (swap_y, 3), 4: (swap_x, 1), 6: (swap_x, 3)}.get(k)
        if swap:
            chunks[16 - k], *parts = after(chunks[16 - k], *parts)
            held = jnp.concatenate(parts) if len(parts) > 1 else parts[0]
            parts.append(swap[0](held, swap[1]))
    y1, y3, x1, x3 = parts[1:]

    piece = jax.ShapeDtypeStruct((tokens // 2, width // 2), F32)
    send_a, send_b, keep_a, keep_b, rows_out = pl.pallas_call(
        grad_inputs_kernel,
        out_shape=[piece] * 4 + [jax.ShapeDtypeStruct((tokens, columns), BF16)],
        in_specs=[SMEM] + [VMEM] * 17,
        out_specs=[VMEM] * 5,
        compiler_params=pltpu.CompilerParams(vmem_limit_bytes=12 << 20),
        cost_estimate=pl.CostEstimate(
            flops=2 * tokens * width * columns, bytes_accessed=6 << 20, transcendentals=0
        ),
        name="grad_inputs",
    )(jnp.stack([depth, col]), *chunks, weight)
    got_a, got_b = swap_x(send_a, 1), swap_x(send_b, 3)

    half = jax.ShapeDtypeStruct((width // 2, columns), F32)
    send_w, keep_w = pl.pallas_call(
        grad_weight_kernel,
        out_shape=[half] * 2,
        in_specs=[SMEM] + [VMEM] * 6,
        out_specs=[VMEM] * 2,
        scratch_shapes=[pltpu.VMEM((tokens, width), BF16), pltpu.VMEM((width, columns), F32)],
        compiler_params=pltpu.CompilerParams(vmem_limit_bytes=20 << 20),
        cost_estimate=pl.CostEstimate(
            flops=2 * tokens * width * columns, bytes_accessed=7 << 20, transcendentals=0
        ),
        name="grad_weight",
    )(row.reshape(1), rows_out, parts[0], y1, y3, x1, x3)

    rows = width // 4
    got_w = swap_row(send_w, 1)
    sum_w = keep_w + got_w
    got_w2 = swap_row(sum_w[rows:], 2)

    quarter = tokens // 4
    got_a, got_b, sum_w = after(got_a, got_b, sum_w)
    sum_a, sum_b = keep_a + got_a, keep_b + got_b
    got_a, got_b = swap_x(sum_a[quarter:], 3), swap_x(sum_b[quarter:], 1)

    sum_a = (sum_a[:quarter] + got_a).reshape(4, block, width // 2)
    sum_b = (sum_b[:quarter] + got_b).reshape(4, block, width // 2)
    got_a = swap_y(jnp.concatenate([sum_a[1:2], sum_a[3:4]]), 1)
    got_b = swap_y(sum_b[2:4], 3)
    sum_a0, sum_a3 = sum_a[0] + got_a[0], sum_a[2] + got_a[1]
    sum_b0, sum_b1 = sum_b[0] + got_b[0], sum_b[1] + got_b[1]
    got_a, got_b = swap_y(sum_a3, 3), swap_y(sum_b1, 1)
    grad_inputs = jnp.concatenate([sum_a0 + got_a, sum_b0 + got_b], axis=1)
    grad_weight = sum_w[:rows] + got_w2
    return grad_inputs.astype(BF16), grad_weight.astype(BF16)


def solution(mesh):
    placed = (P(("row", "col"), "depth"), P("depth", "col"), P(("row", "depth"), "col"))
    return jax.shard_map(
        per_device,
        mesh=mesh,
        in_specs=placed,
        out_specs=(P(("row", "col"), "depth"), P(("depth", "row"), "col")),
        check_vma=False,
    )
```

```python
import jax
import jax.numpy as jnp
from jax import lax
from jax.experimental import pallas as pl
from jax.experimental.pallas import tpu as pltpu
from jax.sharding import PartitionSpec as P

F32 = jnp.float32
BF16 = jnp.bfloat16
VMEM = pl.BlockSpec(memory_space=pltpu.VMEM)
SMEM = pl.BlockSpec(memory_space=pltpu.SMEM)
ORDER = (0, 1, 3, 2)


def swap_x(value, j):
    return lax.ppermute(value, "col", [(i, i ^ j) for i in range(16)])


def swap_y(value, j):
    return lax.ppermute(value, "col", [(i, i ^ (4 * j)) for i in range(16)])


def swap_row(value, j):
    return lax.ppermute(value, "row", [(i, i ^ j) for i in range(4)])


def grad_inputs_kernel(col_ref, grad_lo, grad_hi, weight_ref, send_a, send_b, keep_a, keep_b, rows):
    block = grad_lo.shape[0] // 16
    half, cut = weight_ref.shape[0] // 2, grad_lo.shape[1]
    for at in range(16):
        j = ORDER[at % 4] * 4 + at // 4
        source = pl.multiple_of(jnp.bitwise_xor(col_ref[0], j) * block, block)
        rows[pl.ds(at * block, block), :cut] = grad_lo[pl.ds(source, block), :]
        rows[pl.ds(at * block, block), cut:] = grad_hi[pl.ds(source, block), :]
    quarter = 4 * block
    for out_half, (sent, kept, sends, keeps) in enumerate(
        ((send_a, keep_a, (1, 2), (0, 3)), (send_b, keep_b, (3, 2), (0, 1)))
    ):
        part = lax.dot_general(
            rows[...],
            weight_ref[pl.ds(out_half * half, half), :],
            (((1,), (1,)), ((), ())),
            preferred_element_type=F32,
        )
        for ref, order in ((sent, sends), (kept, keeps)):
            for slot, jx in enumerate(order):
                ref[pl.ds(slot * quarter, quarter), :] = part[jx * quarter : (jx + 1) * quarter]


def grad_weight_kernel(row_ref, grad_lo, grad_hi, in_lo, in_hi, sent, kept, total):
    height, cut = in_lo.shape[1], grad_lo.shape[1]
    for i, tokens in enumerate((in_lo, in_hi)):
        for grads, columns in ((grad_lo, slice(0, cut)), (grad_hi, slice(cut, None))):
            total[pl.ds(i * height, height), columns] = lax.dot_general(
                tokens[...], grads[...], (((0,), (0,)), ((), ())), preferred_element_type=F32
            )
    rows = total.shape[0] // 4
    for jy in range(2):
        for jc, ref in ((1, sent), (0, kept)):
            source = jnp.bitwise_xor(row_ref[0], jy * 2 + jc) * rows
            ref[pl.ds(jy * rows, rows), :] = total[pl.ds(pl.multiple_of(source, rows), rows), :]


def after(*values):
    return lax.optimization_barrier(values)


def per_device(inputs, weight, grad_out):
    block, width = inputs.shape
    columns = weight.shape[1]
    tokens = block * 16
    col, row = lax.axis_index("col"), lax.axis_index("row")
    cut = columns * 5 // 9
    grads = [
        lax.all_gather(part, "depth", axis=0, tiled=True)
        for part in (grad_out[:, :cut], grad_out[:, cut:])
    ]
    gathered = [
        lax.all_gather(part, "col", axis=0, tiled=True)
        for part in (inputs[:, : width // 2], inputs[:, width // 2 :])
    ]

    piece = jax.ShapeDtypeStruct((tokens // 2, width // 2), F32)
    send_a, send_b, keep_a, keep_b = pl.pallas_call(
        grad_inputs_kernel,
        out_shape=[piece] * 4,
        in_specs=[SMEM] + [VMEM] * 3,
        out_specs=[VMEM] * 4,
        scratch_shapes=[pltpu.VMEM((tokens, columns), BF16)],
        compiler_params=pltpu.CompilerParams(vmem_limit_bytes=12 << 20),
        cost_estimate=pl.CostEstimate(
            flops=2 * tokens * width * columns, bytes_accessed=6 << 20, transcendentals=0
        ),
        name="grad_inputs",
    )(col.reshape(1), *grads, weight)
    got_a, got_b = swap_x(send_a, 1), swap_x(send_b, 3)

    half = jax.ShapeDtypeStruct((width // 2, columns), F32)
    send_w, keep_w = pl.pallas_call(
        grad_weight_kernel,
        out_shape=[half] * 2,
        in_specs=[SMEM] + [VMEM] * 4,
        out_specs=[VMEM] * 2,
        scratch_shapes=[pltpu.VMEM((width, columns), F32)],
        compiler_params=pltpu.CompilerParams(vmem_limit_bytes=20 << 20),
        cost_estimate=pl.CostEstimate(
            flops=2 * tokens * width * columns, bytes_accessed=7 << 20, transcendentals=0
        ),
        name="grad_weight",
    )(row.reshape(1), *grads, *gathered)

    rows = width // 4
    got_w = swap_row(send_w, 1)
    sum_w = keep_w[rows:] + got_w[rows:]
    got_w2 = swap_row(sum_w, 2)

    quarter = tokens // 4
    got_a, got_b, sum_w = after(got_a, got_b, sum_w)
    sum_a, sum_b = keep_a + got_a, keep_b + got_b
    got_a, got_b = swap_x(sum_a[quarter:], 3), swap_x(sum_b[quarter:], 1)

    sum_a = (sum_a[:quarter] + got_a).reshape(4, block, width // 2)
    sum_b = (sum_b[:quarter] + got_b).reshape(4, block, width // 2)
    got_a = swap_y(jnp.concatenate([sum_a[1:2], sum_a[3:4]]), 1)
    got_b = swap_y(sum_b[2:4], 3)
    sum_a0, sum_a3 = sum_a[0] + got_a[0], sum_a[2] + got_a[1]
    sum_b0, sum_b1 = sum_b[0] + got_b[0], sum_b[1] + got_b[1]
    got_a, got_b = swap_y(sum_a3, 3), swap_y(sum_b1, 1)
    grad_inputs = jnp.concatenate([sum_a0 + got_a, sum_b0 + got_b], axis=1)
    grad_weight = keep_w[:rows] + got_w[:rows] + got_w2
    return grad_inputs.astype(BF16), grad_weight.astype(BF16)


def solution(mesh):
    placed = (P(("row", "col"), "depth"), P("depth", "col"), P(("row", "depth"), "col"))
    return jax.shard_map(
        per_device,
        mesh=mesh,
        in_specs=placed,
        out_specs=(P(("row", "col"), "depth"), P(("depth", "row"), "col")),
        check_vma=False,
    )
```

```python
import jax
import jax.numpy as jnp
from jax import lax
from jax.experimental import pallas as pl
from jax.experimental.pallas import tpu as pltpu
from jax.sharding import PartitionSpec as P

F32 = jnp.float32
BF16 = jnp.bfloat16
VMEM = pl.BlockSpec(memory_space=pltpu.VMEM)
SMEM = pl.BlockSpec(memory_space=pltpu.SMEM)
ORDER = (0, 1, 3, 2)


def swap_x(value, j):
    return lax.ppermute(value, "col", [(i, i ^ j) for i in range(16)])


def swap_y(value, j):
    return lax.ppermute(value, "col", [(i, i ^ (4 * j)) for i in range(16)])


def swap_row(value, j):
    return lax.ppermute(value, "row", [(i, i ^ j) for i in range(4)])


def grad_inputs_kernel(col_ref, grad_lo, grad_hi, weight_ref, send_a, send_b, keep_a, keep_b, first, rows):
    block = grad_lo.shape[0] // 16
    half, cut = weight_ref.shape[0] // 2, grad_lo.shape[1]
    for at in range(16):
        j = ORDER[at % 4] * 4 + at // 4
        source = pl.multiple_of(jnp.bitwise_xor(col_ref[0], j) * block, block)
        rows[pl.ds(at * block, block), :cut] = grad_lo[pl.ds(source, block), :]
        rows[pl.ds(at * block, block), cut:] = grad_hi[pl.ds(source, block), :]
    first[...] = jnp.zeros_like(first)
    quarter = 4 * block
    for out_half, (sent, kept, sends, keeps) in enumerate(
        ((send_a, keep_a, (1, 2), (0, 3)), (send_b, keep_b, (3, 2), (0, 1)))
    ):
        part = lax.dot_general(
            rows[...],
            weight_ref[pl.ds(out_half * half, half), :],
            (((1,), (1,)), ((), ())),
            preferred_element_type=F32,
        )
        for ref, order in ((sent, sends), (kept, keeps)):
            for slot, jx in enumerate(order):
                ref[pl.ds(slot * quarter, quarter), :] = part[jx * quarter : (jx + 1) * quarter]


def grad_weight_kernel(row_ref, _, grad_lo, grad_hi, tokens, sent, kept, total):
    cut = grad_lo.shape[1]
    for grads, columns in ((grad_lo, slice(0, cut)), (grad_hi, slice(cut, None))):
        total[:, columns] = lax.dot_general(
            tokens[...], grads[...], (((0,), (0,)), ((), ())), preferred_element_type=F32
        )
    rows = total.shape[0] // 4
    for jy in range(2):
        for jc, ref in ((1, sent), (0, kept)):
            source = jnp.bitwise_xor(row_ref[0], jy * 2 + jc) * rows
            ref[pl.ds(jy * rows, rows), :] = total[pl.ds(pl.multiple_of(source, rows), rows), :]


def after(*values):
    return lax.optimization_barrier(values)


def per_device(inputs, weight, grad_out):
    block, width = inputs.shape
    columns = weight.shape[1]
    tokens = block * 16
    col, row = lax.axis_index("col"), lax.axis_index("row")
    cut = columns * 5 // 9
    grads = [
        lax.all_gather(part, "depth", axis=0, tiled=True)
        for part in (grad_out[:, :cut], grad_out[:, cut:])
    ]
    gathered = lax.all_gather(inputs, "col", axis=0, tiled=True)

    piece = jax.ShapeDtypeStruct((tokens // 2, width // 2), F32)
    send_a, send_b, keep_a, keep_b, first = pl.pallas_call(
        grad_inputs_kernel,
        out_shape=[piece] * 4 + [jax.ShapeDtypeStruct((8, 128), F32)],
        in_specs=[SMEM] + [VMEM] * 3,
        out_specs=[VMEM] * 5,
        scratch_shapes=[pltpu.VMEM((tokens, columns), BF16)],
        compiler_params=pltpu.CompilerParams(vmem_limit_bytes=12 << 20),
        cost_estimate=pl.CostEstimate(
            flops=2 * tokens * width * columns, bytes_accessed=6 << 20, transcendentals=0
        ),
        name="grad_inputs",
    )(col.reshape(1), *grads, weight)
    got_a, got_b = swap_x(send_a, 1), swap_x(send_b, 3)

    half = jax.ShapeDtypeStruct((width // 2, columns), F32)
    send_w, keep_w = pl.pallas_call(
        grad_weight_kernel,
        out_shape=[half] * 2,
        in_specs=[SMEM] + [VMEM] * 4,
        out_specs=[VMEM] * 2,
        scratch_shapes=[pltpu.VMEM((width, columns), F32)],
        compiler_params=pltpu.CompilerParams(vmem_limit_bytes=14 << 20),
        cost_estimate=pl.CostEstimate(
            flops=2 * tokens * width * columns, bytes_accessed=7 << 20, transcendentals=0
        ),
        name="grad_weight",
    )(row.reshape(1), first, *grads, gathered)

    rows = width // 4
    got_w = swap_row(send_w, 1)
    sum_w = keep_w[rows:] + got_w[rows:]
    got_w2 = swap_row(sum_w, 2)

    quarter = tokens // 4
    got_a, got_b, sum_w = after(got_a, got_b, sum_w)
    sum_a, sum_b = keep_a + got_a, keep_b + got_b
    got_a, got_b = swap_x(sum_a[quarter:], 3), swap_x(sum_b[quarter:], 1)

    got_a, got_b, got_w2 = after(got_a, got_b, got_w2)
    sum_a = (sum_a[:quarter] + got_a).reshape(4, block, width // 2)
    sum_b = (sum_b[:quarter] + got_b).reshape(4, block, width // 2)
    got_a = swap_y(jnp.concatenate([sum_a[1:2], sum_a[3:4]]), 1)
    got_b = swap_y(sum_b[2:4], 3)
    sum_a0, sum_a3 = sum_a[0] + got_a[0], sum_a[2] + got_a[1]
    sum_b0, sum_b1 = sum_b[0] + got_b[0], sum_b[1] + got_b[1]
    got_a, got_b = swap_y(sum_a3, 3), swap_y(sum_b1, 1)
    grad_inputs = jnp.concatenate([sum_a0 + got_a, sum_b0 + got_b], axis=1)
    grad_weight = keep_w[:rows] + got_w[:rows] + got_w2
    return grad_inputs.astype(BF16), grad_weight.astype(BF16)


def solution(mesh):
    placed = (P(("row", "col"), "depth"), P("depth", "col"), P(("row", "depth"), "col"))
    return jax.shard_map(
        per_device,
        mesh=mesh,
        in_specs=placed,
        out_specs=(P(("row", "col"), "depth"), P(("depth", "row"), "col")),
        check_vma=False,
    )
```

```python
import jax
import jax.numpy as jnp
from jax import lax
from jax.experimental import pallas as pl
from jax.experimental.pallas import tpu as pltpu
from jax.sharding import PartitionSpec as P

F32 = jnp.float32
BF16 = jnp.bfloat16
VMEM = pl.BlockSpec(memory_space=pltpu.VMEM)
SMEM = pl.BlockSpec(memory_space=pltpu.SMEM)
ORDER = (0, 1, 3, 2)


def swap_x(value, j):
    return lax.ppermute(value, "col", [(i, i ^ j) for i in range(16)])


def swap_y(value, j):
    return lax.ppermute(value, "col", [(i, i ^ (4 * j)) for i in range(16)])


def swap_row(value, j):
    return lax.ppermute(value, "row", [(i, i ^ j) for i in range(4)])


def spread(depth, chunks, block, into, place):
    parity = jnp.bitwise_and(depth, 1)
    for ref, own, lead in zip(chunks, (1, 0, 0), (0, 0, ref_blocks(chunks[1], block))):
        for k in range(ref_blocks(ref, block)):
            source = 2 * (lead + k) + (parity if own else 1 - parity)
            at = pl.multiple_of(place(source) * block, block)
            into[pl.ds(at, block), :] = ref[pl.ds(k * block, block), :]


def ref_blocks(ref, block):
    return ref.shape[0] // block


def grad_inputs_kernel(place_ref, own, near, far, weight_ref, send_a, send_b, keep_a, keep_b, rows):
    block = own.shape[0] // 8
    half = weight_ref.shape[0] // 2

    def place(source):
        j = jnp.bitwise_xor(source, place_ref[1])
        jx, jy = jnp.bitwise_and(j, 3), jnp.right_shift(j, 2)
        return jx * 4 + jnp.bitwise_xor(jy, jnp.right_shift(jy, 1))

    spread(place_ref[0], (own, near, far), block, rows, place)
    quarter = 4 * block
    for out_half, (sent, kept, sends, keeps) in enumerate(
        ((send_a, keep_a, (1, 2), (0, 3)), (send_b, keep_b, (3, 2), (0, 1)))
    ):
        part = lax.dot_general(
            rows[...],
            weight_ref[pl.ds(out_half * half, half), :],
            (((1,), (1,)), ((), ())),
            preferred_element_type=F32,
        )
        for ref, order in ((sent, sends), (kept, keeps)):
            for slot, jx in enumerate(order):
                ref[pl.ds(slot * quarter, quarter), :] = part[jx * quarter : (jx + 1) * quarter]


def grad_weight_kernel(place_ref, _a, _b, own, near, far, tokens, sent, kept, grads, total):
    spread(place_ref[0], (own, near, far), own.shape[0] // 8, grads, lambda source: source)
    total[...] = lax.dot_general(
        tokens[...], grads[...], (((0,), (0,)), ((), ())), preferred_element_type=F32
    )
    rows = total.shape[0] // 4
    for jy in range(2):
        for jc, ref in ((1, sent), (0, kept)):
            source = jnp.bitwise_xor(place_ref[1], jy * 2 + jc) * rows
            ref[pl.ds(jy * rows, rows), :] = total[pl.ds(pl.multiple_of(source, rows), rows), :]


def after(*values):
    return lax.optimization_barrier(values)


def per_device(inputs, weight, grad_out):
    block, width = inputs.shape
    columns = weight.shape[1]
    tokens = block * 16
    depth, col, row = (lax.axis_index(a) for a in ("depth", "col", "row"))
    own = lax.all_gather(
        grad_out,
        "depth",
        axis=0,
        tiled=True,
        axis_index_groups=[list(range(parity, 16, 2)) for parity in range(2)],
    )
    near = lax.ppermute(own[: tokens // 4], "depth", [(i, i ^ 1) for i in range(16)])
    far = lax.ppermute(own[tokens // 4 :], "depth", [(i, ((i + 1) ^ 1) - 1 & 15) for i in range(16)])
    grads = (own, near, far)
    gathered = lax.all_gather(inputs, "col", axis=0, tiled=True)

    piece = jax.ShapeDtypeStruct((tokens // 2, width // 2), F32)
    send_a, send_b, keep_a, keep_b = pl.pallas_call(
        grad_inputs_kernel,
        out_shape=[piece] * 4,
        in_specs=[SMEM] + [VMEM] * 4,
        out_specs=[VMEM] * 4,
        scratch_shapes=[pltpu.VMEM((tokens, columns), BF16)],
        compiler_params=pltpu.CompilerParams(vmem_limit_bytes=12 << 20),
        cost_estimate=pl.CostEstimate(
            flops=2 * tokens * width * columns, bytes_accessed=6 << 20, transcendentals=0
        ),
        name="grad_inputs",
    )(jnp.stack([depth, col]), *grads, weight)
    got_a, got_b = swap_x(send_a, 1), swap_x(send_b, 3)

    quarter = tokens // 4
    sum_a, sum_b = keep_a + got_a, keep_b + got_b
    got_a, got_b = swap_x(sum_a[quarter:], 3), swap_x(sum_b[quarter:], 1)

    half = jax.ShapeDtypeStruct((width // 2, columns), F32)
    send_w, keep_w = pl.pallas_call(
        grad_weight_kernel,
        out_shape=[half] * 2,
        in_specs=[SMEM] + [pl.BlockSpec(memory_space=pl.ANY)] * 2 + [VMEM] * 4,
        out_specs=[VMEM] * 2,
        scratch_shapes=[pltpu.VMEM((tokens, columns), BF16), pltpu.VMEM((width, columns), F32)],
        compiler_params=pltpu.CompilerParams(vmem_limit_bytes=16 << 20),
        cost_estimate=pl.CostEstimate(
            flops=2 * tokens * width * columns, bytes_accessed=7 << 20, transcendentals=0
        ),
        name="grad_weight",
    )(jnp.stack([depth, row]), got_a, got_b, *grads, gathered)

    rows = width // 4
    got_w = swap_row(send_w, 1)
    sum_w = keep_w[rows:] + got_w[rows:]
    got_w2 = swap_row(sum_w, 2)

    sum_a = (sum_a[:quarter] + got_a).reshape(4, block, width // 2)
    sum_b = (sum_b[:quarter] + got_b).reshape(4, block, width // 2)
    got_a = swap_y(jnp.concatenate([sum_a[1:2], sum_a[3:4]]), 1)
    got_b = swap_y(sum_b[2:4], 3)
    sum_a0, sum_a3 = sum_a[0] + got_a[0], sum_a[2] + got_a[1]
    sum_b0, sum_b1 = sum_b[0] + got_b[0], sum_b[1] + got_b[1]
    got_a, got_b = swap_y(sum_a3, 3), swap_y(sum_b1, 1)
    grad_inputs = jnp.concatenate([sum_a0 + got_a, sum_b0 + got_b], axis=1)
    grad_weight = keep_w[:rows] + got_w[:rows] + got_w2
    return grad_inputs.astype(BF16), grad_weight.astype(BF16)


def solution(mesh):
    placed = (P(("row", "col"), "depth"), P("depth", "col"), P(("row", "depth"), "col"))
    return jax.shard_map(
        per_device,
        mesh=mesh,
        in_specs=placed,
        out_specs=(P(("row", "col"), "depth"), P(("depth", "row"), "col")),
        check_vma=False,
    )
```

```python
import jax
import jax.numpy as jnp
from jax import lax
from jax.experimental import pallas as pl
from jax.experimental.pallas import tpu as pltpu
from jax.sharding import PartitionSpec as P

F32 = jnp.float32
BF16 = jnp.bfloat16
VMEM = pl.BlockSpec(memory_space=pltpu.VMEM)
SMEM = pl.BlockSpec(memory_space=pltpu.SMEM)
ORDER = (0, 1, 3, 2)


def swap_x(value, j):
    return lax.ppermute(value, "col", [(i, i ^ j) for i in range(16)])


def swap_y(value, j):
    return lax.ppermute(value, "col", [(i, i ^ (4 * j)) for i in range(16)])


def swap_row(value, j):
    return lax.ppermute(value, "row", [(i, i ^ j) for i in range(4)])


def spread(depth, chunks, block, into, place):
    parity = jnp.bitwise_and(depth, 1)
    for ref, own, lead in zip(chunks, (1, 0, 0), (0, 0, ref_blocks(chunks[1], block))):
        for k in range(ref_blocks(ref, block)):
            source = 2 * (lead + k) + (parity if own else 1 - parity)
            at = pl.multiple_of(place(source) * block, block)
            into[pl.ds(at, block), :] = ref[pl.ds(k * block, block), :]


def ref_blocks(ref, block):
    return ref.shape[0] // block


def grad_inputs_kernel(place_ref, own, near, far, weight_ref, send_a, send_b, keep_a, keep_b, rows):
    block = own.shape[0] // 8
    half = weight_ref.shape[0] // 2

    def place(source):
        j = jnp.bitwise_xor(source, place_ref[1])
        jx, jy = jnp.bitwise_and(j, 3), jnp.right_shift(j, 2)
        return jx * 4 + jnp.bitwise_xor(jy, jnp.right_shift(jy, 1))

    spread(place_ref[0], (own, near, far), block, rows, place)
    quarter = 4 * block
    for out_half, (sent, kept, sends, keeps) in enumerate(
        ((send_a, keep_a, (1, 2), (0, 3)), (send_b, keep_b, (3, 2), (0, 1)))
    ):
        part = lax.dot_general(
            rows[...],
            weight_ref[pl.ds(out_half * half, half), :],
            (((1,), (1,)), ((), ())),
            preferred_element_type=F32,
        )
        for ref, order in ((sent, sends), (kept, keeps)):
            for slot, jx in enumerate(order):
                ref[pl.ds(slot * quarter, quarter), :] = part[jx * quarter : (jx + 1) * quarter]


def grad_weight_kernel(place_ref, _a, _b, own, near, far, tokens, sent, kept, grads, total):
    spread(place_ref[0], (own, near, far), own.shape[0] // 8, grads, lambda source: source)
    total[...] = lax.dot_general(
        tokens[...], grads[...], (((0,), (0,)), ((), ())), preferred_element_type=F32
    )
    rows = total.shape[0] // 4
    for jy in range(2):
        for jc, ref in ((1, sent), (0, kept)):
            source = jnp.bitwise_xor(place_ref[1], jy * 2 + jc) * rows
            ref[pl.ds(jy * rows, rows), :] = total[pl.ds(pl.multiple_of(source, rows), rows), :]


def after(*values):
    return lax.optimization_barrier(values)


def per_device(inputs, weight, grad_out):
    block, width = inputs.shape
    columns = weight.shape[1]
    tokens = block * 16
    depth, col, row = (lax.axis_index(a) for a in ("depth", "col", "row"))
    own = lax.all_gather(
        grad_out,
        "depth",
        axis=0,
        tiled=True,
        axis_index_groups=[list(range(parity, 16, 2)) for parity in range(2)],
    )
    near = lax.ppermute(own[: tokens // 4], "depth", [(i, i ^ 1) for i in range(16)])
    far = lax.ppermute(own[tokens // 4 :], "depth", [(i, ((i + 1) ^ 1) - 1 & 15) for i in range(16)])
    grads = (own, near, far)
    gathered = lax.all_gather(inputs, "col", axis=0, tiled=True)

    piece = jax.ShapeDtypeStruct((tokens // 2, width // 2), F32)
    send_a, send_b, keep_a, keep_b = pl.pallas_call(
        grad_inputs_kernel,
        out_shape=[piece] * 4,
        in_specs=[SMEM] + [VMEM] * 4,
        out_specs=[VMEM] * 4,
        scratch_shapes=[pltpu.VMEM((tokens, columns), BF16)],
        compiler_params=pltpu.CompilerParams(vmem_limit_bytes=7 << 20),
        cost_estimate=pl.CostEstimate(
            flops=2 * tokens * width * columns, bytes_accessed=6 << 20, transcendentals=0
        ),
        name="grad_inputs",
    )(jnp.stack([depth, col]), *grads, weight)
    got_a, got_b = swap_x(send_a, 1), swap_x(send_b, 3)

    half = jax.ShapeDtypeStruct((width // 2, columns), F32)
    send_w, keep_w = pl.pallas_call(
        grad_weight_kernel,
        out_shape=[half] * 2,
        in_specs=[SMEM] + [pl.BlockSpec(memory_space=pl.ANY)] * 2 + [VMEM] * 4,
        out_specs=[VMEM] * 2,
        scratch_shapes=[pltpu.VMEM((tokens, columns), BF16), pltpu.VMEM((width, columns), F32)],
        compiler_params=pltpu.CompilerParams(vmem_limit_bytes=9 << 20),
        cost_estimate=pl.CostEstimate(
            flops=2 * tokens * width * columns, bytes_accessed=7 << 20, transcendentals=0
        ),
        name="grad_weight",
    )(jnp.stack([depth, row]), got_a, got_b, *grads, gathered)

    rows = width // 4
    got_w = swap_row(send_w, 1)
    sum_w = keep_w[rows:] + got_w[rows:]
    got_w2 = swap_row(sum_w, 2)

    quarter = tokens // 4
    sum_a, sum_b = keep_a + got_a, keep_b + got_b
    got_a, got_b = swap_x(sum_a[quarter:], 3), swap_x(sum_b[quarter:], 1)

    got_a, got_b, sum_w = after(got_a, got_b, sum_w)
    sum_a = (sum_a[:quarter] + got_a).reshape(4, block, width // 2)
    sum_b = (sum_b[:quarter] + got_b).reshape(4, block, width // 2)
    got_a = swap_y(jnp.concatenate([sum_a[1:2], sum_a[3:4]]), 1)
    got_b = swap_y(sum_b[2:4], 3)
    sum_a0, sum_a3 = sum_a[0] + got_a[0], sum_a[2] + got_a[1]
    sum_b0, sum_b1 = sum_b[0] + got_b[0], sum_b[1] + got_b[1]
    sum_a3, sum_b1, got_w2 = after(sum_a3, sum_b1, got_w2)
    got_a, got_b = swap_y(sum_a3, 3), swap_y(sum_b1, 1)
    grad_inputs = jnp.concatenate([sum_a0 + got_a, sum_b0 + got_b], axis=1)
    grad_weight = keep_w[:rows] + got_w[:rows] + got_w2
    return grad_inputs.astype(BF16), grad_weight.astype(BF16)


def solution(mesh):
    placed = (P(("row", "col"), "depth"), P("depth", "col"), P(("row", "depth"), "col"))
    return jax.shard_map(
        per_device,
        mesh=mesh,
        in_specs=placed,
        out_specs=(P(("row", "col"), "depth"), P(("depth", "row"), "col")),
        check_vma=False,
    )
```

```python
import jax
import jax.numpy as jnp
from jax import lax
from jax.experimental import pallas as pl
from jax.experimental.pallas import tpu as pltpu
from jax.sharding import PartitionSpec as P

F32 = jnp.float32
BF16 = jnp.bfloat16
VMEM = pl.BlockSpec(memory_space=pltpu.VMEM)
SMEM = pl.BlockSpec(memory_space=pltpu.SMEM)
ORDER = (0, 1, 3, 2)


def swap_x(value, j):
    return lax.ppermute(value, "col", [(i, i ^ j) for i in range(16)])


def swap_y(value, j):
    return lax.ppermute(value, "col", [(i, i ^ (4 * j)) for i in range(16)])


def swap_row(value, j):
    return lax.ppermute(value, "row", [(i, i ^ j) for i in range(4)])


def grad_inputs_kernel(place_ref, own, near, far, weight_ref, send_a, send_b, keep_a, keep_b, rows):
    block = own.shape[0] // 8
    half = weight_ref.shape[0] // 2

    parity = jnp.bitwise_and(place_ref[0], 1)
    for ref, first, odd in ((own, 0, parity), (near, 0, 1 - parity), (far, 8, 1 - parity)):
        for k in range(ref.shape[0] // block):
            j = jnp.bitwise_xor(first + 2 * k + odd, place_ref[1])
            jx, jy = jnp.bitwise_and(j, 3), jnp.right_shift(j, 2)
            at = jx * 4 + jnp.bitwise_xor(jy, jnp.right_shift(jy, 1))
            rows[pl.ds(pl.multiple_of(at * block, block), block), :] = ref[pl.ds(k * block, block), :]
    quarter = 4 * block
    for out_half, (sent, kept, sends, keeps) in enumerate(
        ((send_a, keep_a, (1, 2), (0, 3)), (send_b, keep_b, (3, 2), (0, 1)))
    ):
        part = lax.dot_general(
            rows[...],
            weight_ref[pl.ds(out_half * half, half), :],
            (((1,), (1,)), ((), ())),
            preferred_element_type=F32,
        )
        for ref, order in ((sent, sends), (kept, keeps)):
            for slot, jx in enumerate(order):
                ref[pl.ds(slot * quarter, quarter), :] = part[jx * quarter : (jx + 1) * quarter]


def grad_weight_kernel(row_ref, grads, x0, x1, x2, x3, sent, kept, tokens, total):
    for jx, ref in enumerate((x0, x1, x2, x3)):
        tokens[pl.ds(jx * ref.shape[0], ref.shape[0]), :] = ref[...]
    total[...] = lax.dot_general(
        tokens[...], grads[...], (((0,), (0,)), ((), ())), preferred_element_type=F32
    )
    rows = total.shape[0] // 4
    for jy in range(2):
        for jc, ref in ((1, sent), (0, kept)):
            source = jnp.bitwise_xor(row_ref[0], jy * 2 + jc) * rows
            ref[pl.ds(jy * rows, rows), :] = total[pl.ds(pl.multiple_of(source, rows), rows), :]


def after(*values):
    return lax.optimization_barrier(values)


def per_device(inputs, weight, grad_out):
    block, width = inputs.shape
    columns = weight.shape[1]
    tokens = block * 16
    depth, col, row = (lax.axis_index(a) for a in ("depth", "col", "row"))
    ring = [inputs] + [swap_y(inputs, j) for j in ORDER[1:]]
    own = lax.all_gather(
        grad_out,
        "depth",
        axis=0,
        tiled=True,
        axis_index_groups=[list(range(parity, 16, 2)) for parity in range(2)],
    )
    near = lax.ppermute(own[: tokens // 4], "depth", [(i, i ^ 1) for i in range(16)])
    far = lax.ppermute(own[tokens // 4 :], "depth", [(i, ((i + 1) ^ 1) - 1 & 15) for i in range(16)])
    x0 = jnp.concatenate(ring)
    x1, x3 = swap_x(x0, 1), swap_x(x0, 3)
    x2 = swap_x(x1, 3)

    piece = jax.ShapeDtypeStruct((tokens // 2, width // 2), F32)
    send_a, send_b, keep_a, keep_b, grads = pl.pallas_call(
        grad_inputs_kernel,
        out_shape=[piece] * 4 + [jax.ShapeDtypeStruct((tokens, columns), BF16)],
        in_specs=[SMEM] + [VMEM] * 4,
        out_specs=[VMEM] * 5,
        compiler_params=pltpu.CompilerParams(vmem_limit_bytes=7 << 20),
        cost_estimate=pl.CostEstimate(
            flops=2 * tokens * width * columns, bytes_accessed=6 << 20, transcendentals=0
        ),
        name="grad_inputs",
    )(jnp.stack([depth, col]), own, near, far, weight)
    got_a, got_b = swap_x(send_a, 1), swap_x(send_b, 3)

    half = jax.ShapeDtypeStruct((width // 2, columns), F32)
    send_w, keep_w = pl.pallas_call(
        grad_weight_kernel,
        out_shape=[half] * 2,
        in_specs=[SMEM] + [VMEM] * 5,
        out_specs=[VMEM] * 2,
        scratch_shapes=[pltpu.VMEM((tokens, width), BF16), pltpu.VMEM((width, columns), F32)],
        compiler_params=pltpu.CompilerParams(vmem_limit_bytes=9 << 20),
        cost_estimate=pl.CostEstimate(
            flops=2 * tokens * width * columns, bytes_accessed=7 << 20, transcendentals=0
        ),
        name="grad_weight",
    )(row.reshape(1), grads, x0, x1, x2, x3)

    rows = width // 4
    got_w = swap_row(send_w, 1)
    sum_w = keep_w[rows:] + got_w[rows:]
    got_w2 = swap_row(sum_w, 2)

    quarter = tokens // 4
    sum_a, sum_b = keep_a + got_a, keep_b + got_b
    got_a, got_b = swap_x(sum_a[quarter:], 3), swap_x(sum_b[quarter:], 1)

    got_a, got_b, sum_w = after(got_a, got_b, sum_w)
    sum_a = (sum_a[:quarter] + got_a).reshape(4, block, width // 2)
    sum_b = (sum_b[:quarter] + got_b).reshape(4, block, width // 2)
    got_a = swap_y(jnp.concatenate([sum_a[1:2], sum_a[3:4]]), 1)
    got_b = swap_y(sum_b[2:4], 3)
    sum_a0, sum_a3 = sum_a[0] + got_a[0], sum_a[2] + got_a[1]
    sum_b0, sum_b1 = sum_b[0] + got_b[0], sum_b[1] + got_b[1]
    sum_a3, sum_b1, got_w2 = after(sum_a3, sum_b1, got_w2)
    got_a, got_b = swap_y(sum_a3, 3), swap_y(sum_b1, 1)
    grad_inputs = jnp.concatenate([sum_a0 + got_a, sum_b0 + got_b], axis=1)
    grad_weight = keep_w[:rows] + got_w[:rows] + got_w2
    return grad_inputs.astype(BF16), grad_weight.astype(BF16)


def solution(mesh):
    placed = (P(("row", "col"), "depth"), P("depth", "col"), P(("row", "depth"), "col"))
    return jax.shard_map(
        per_device,
        mesh=mesh,
        in_specs=placed,
        out_specs=(P(("row", "col"), "depth"), P(("depth", "row"), "col")),
        check_vma=False,
    )
```

```python
import jax
import jax.numpy as jnp
from jax import lax
from jax.experimental import pallas as pl
from jax.experimental.pallas import tpu as pltpu
from jax.sharding import PartitionSpec as P

F32 = jnp.float32
BF16 = jnp.bfloat16
VMEM = pl.BlockSpec(memory_space=pltpu.VMEM)
SMEM = pl.BlockSpec(memory_space=pltpu.SMEM)
ORDER = (0, 1, 3, 2)


def swap_x(value, j):
    return lax.ppermute(value, "col", [(i, i ^ j) for i in range(16)])


def swap_y(value, j):
    return lax.ppermute(value, "col", [(i, i ^ (4 * j)) for i in range(16)])


def swap_row(value, j):
    return lax.ppermute(value, "row", [(i, i ^ j) for i in range(4)])


def encode(value):
    largest = jnp.max(jnp.max(jnp.abs(value), axis=1, keepdims=True), axis=0, keepdims=True)
    power = jnp.clip(jnp.ceil(jnp.log2(jnp.maximum(largest, 1e-30))), -100.0, 100.0)
    scaled = jnp.abs(value) * jnp.exp2(7.5 - power)
    for _ in range(4):
        scaled = scaled * scaled
    rows = jnp.broadcast_to(power, (16, value.shape[1]))
    return jnp.where(value < 0, -scaled, scaled).astype(BF16), rows.astype(BF16)


def decode(ref, start, size):
    tail = ref.shape[0] - 16
    power = ref[tail:, :].astype(F32)[:1, :1]
    code = ref[pl.ds(start, size), :].astype(F32)
    root = jnp.abs(code)
    for _ in range(4):
        root = jnp.sqrt(root)
    root = root * jnp.exp2(power - 7.5)
    return jnp.where(code < 0, -root, root)


def put(ref, value):
    coded, power = encode(value)
    ref[: value.shape[0], :] = coded
    ref[value.shape[0] :, :] = power


def spread(depth, chunks, block, into, place):
    parity = jnp.bitwise_and(depth, 1)
    for ref, own, lead in zip(chunks, (1, 0, 0), (0, 0, 4)):
        for k in range(ref.shape[0] // block):
            source = 2 * (lead + k) + (parity if own else 1 - parity)
            at = pl.multiple_of(place(source) * block, block)
            into[pl.ds(at, block), :] = ref[pl.ds(k * block, block), :]


def grad_inputs_kernel(place_ref, own, near, far, weight_ref, sent, kept, rows):
    block = own.shape[0] // 8

    def place(source):
        j = jnp.bitwise_xor(source, place_ref[1])
        jx, jy = jnp.bitwise_and(j, 3), jnp.right_shift(j, 2)
        slot = jnp.where(jx == 0, 2, jnp.where(jx == 3, 3, jx - 1))
        return slot * 4 + jnp.bitwise_xor(jy, jnp.right_shift(jy, 1))

    spread(place_ref[0], (own, near, far), block, rows, place)
    half = 8 * block
    for at, ref in ((0, sent), (half, kept)):
        part = lax.dot_general(
            rows[pl.ds(at, half), :],
            weight_ref[...],
            (((1,), (1,)), ((), ())),
            preferred_element_type=F32,
        )
        if at:
            ref[...] = part
        else:
            put(ref, part)


def x_stage_kernel(mine, got, sent, kept):
    size = mine.shape[0] // 2
    put(sent, mine[size:, :] + decode(got, size, size))
    kept[...] = mine[:size, :] + decode(got, 0, size)


def y_stage_kernel(mine, got, sent, kept):
    block = mine.shape[0] // 4
    total = mine[...] + decode(got, 0, mine.shape[0])
    put(sent, jnp.concatenate([total[block : 2 * block], total[3 * block :]]))
    kept[:block, :] = total[:block]
    kept[block:, :] = total[2 * block : 3 * block]


def last_stage_kernel(mine, got, sent, kept):
    block = mine.shape[0] // 2
    kept[...] = mine[:block, :] + decode(got, 0, block)
    sent[...] = mine[block:, :] + decode(got, block, block)


def finish_weight_kernel(mine, got, out):
    out[...] = (mine[...] + decode(got, 0, mine.shape[0])).astype(BF16)


def stage(kernel, sent, kept, *operands):
    return pl.pallas_call(
        kernel,
        out_shape=[sent, kept],
        in_specs=[VMEM] * len(operands),
        out_specs=[VMEM] * 2,
        compiler_params=pltpu.CompilerParams(vmem_limit_bytes=10 << 20),
    )(*operands)


def grad_weight_kernel(place_ref, _, own, near, far, tokens, sent, kept, grads, total):
    spread(place_ref[0], (own, near, far), own.shape[0] // 8, grads, lambda source: source)
    total[...] = lax.dot_general(
        tokens[...], grads[...], (((0,), (0,)), ((), ())), preferred_element_type=F32
    )
    rows = total.shape[0] // 4
    for jy in range(2):
        for jc, ref in ((1, sent), (0, kept)):
            source = jnp.bitwise_xor(place_ref[1], jy * 2 + jc) * rows
            ref[pl.ds((1 - jy) * rows, rows), :] = total[pl.ds(pl.multiple_of(source, rows), rows), :]


def sum_weight_kernel(mine, got, sent, kept):
    rows = kept.shape[0]
    put(sent, mine[:rows, :] + got[:rows, :])
    kept[...] = mine[rows:, :] + got[rows:, :]


def per_device(inputs, weight, grad_out):
    block, width = inputs.shape
    columns = weight.shape[1]
    tokens = block * 16
    depth, col, row = (lax.axis_index(a) for a in ("depth", "col", "row"))
    own = lax.all_gather(
        grad_out,
        "depth",
        axis=0,
        tiled=True,
        axis_index_groups=[list(range(parity, 16, 2)) for parity in range(2)],
    )
    near = lax.ppermute(own[: tokens // 4], "depth", [(i, i ^ 1) for i in range(16)])
    far = lax.ppermute(own[tokens // 4 :], "depth", [(i, ((i + 1) ^ 1) - 1 & 15) for i in range(16)])
    grads = (own, near, far)
    gathered = lax.all_gather(inputs, "col", axis=0, tiled=True)

    def plain(rows, cols=width):
        return jax.ShapeDtypeStruct((rows, cols), F32)

    def coded(rows, cols=width):
        return jax.ShapeDtypeStruct((rows + 16, cols), BF16)

    sent, kept = pl.pallas_call(
        grad_inputs_kernel,
        out_shape=[coded(tokens // 2), plain(tokens // 2)],
        in_specs=[SMEM] + [VMEM] * 4,
        out_specs=[VMEM] * 2,
        scratch_shapes=[pltpu.VMEM((tokens, columns), BF16)],
        compiler_params=pltpu.CompilerParams(vmem_limit_bytes=10 << 20),
        cost_estimate=pl.CostEstimate(
            flops=2 * tokens * width * columns, bytes_accessed=6 << 20, transcendentals=0
        ),
        name="grad_inputs",
    )(jnp.stack([depth, col]), *grads, weight)
    got = swap_x(sent, 1)
    sent, kept = stage(x_stage_kernel, coded(tokens // 4), plain(tokens // 4), kept, got)
    got = swap_x(sent, 3)

    send_w, keep_w = pl.pallas_call(
        grad_weight_kernel,
        out_shape=[plain(width // 2, columns)] * 2,
        in_specs=[SMEM, pl.BlockSpec(memory_space=pl.ANY)] + [VMEM] * 4,
        out_specs=[VMEM] * 2,
        scratch_shapes=[pltpu.VMEM((tokens, columns), BF16), pltpu.VMEM((width, columns), F32)],
        compiler_params=pltpu.CompilerParams(vmem_limit_bytes=9 << 20),
        cost_estimate=pl.CostEstimate(
            flops=2 * tokens * width * columns, bytes_accessed=7 << 20, transcendentals=0
        ),
        name="grad_weight",
    )(jnp.stack([depth, row]), got, *grads, gathered)
    rows = width // 4
    got_w = swap_row(send_w, 1)
    sent_w, kept_w = stage(sum_weight_kernel, coded(rows, columns), plain(rows, columns), keep_w, got_w)
    got_w = swap_row(sent_w, 2)

    sent, kept = stage(y_stage_kernel, coded(tokens // 8), plain(tokens // 8), kept, got)
    got = swap_y(sent, 1)
    sent, kept = stage(last_stage_kernel, plain(block), plain(block), kept, got)
    grad_inputs = (kept + swap_y(sent, 3)).astype(BF16)
    grad_weight = pl.pallas_call(
        finish_weight_kernel,
        out_shape=jax.ShapeDtypeStruct((rows, columns), BF16),
        in_specs=[VMEM] * 2,
        out_specs=VMEM,
        compiler_params=pltpu.CompilerParams(vmem_limit_bytes=10 << 20),
    )(kept_w, got_w)
    return grad_inputs, grad_weight


def solution(mesh):
    placed = (P(("row", "col"), "depth"), P("depth", "col"), P(("row", "depth"), "col"))
    return jax.shard_map(
        per_device,
        mesh=mesh,
        in_specs=placed,
        out_specs=(P(("row", "col"), "depth"), P(("depth", "row"), "col")),
        check_vma=False,
    )
```

```python
import jax
import jax.numpy as jnp
from jax import lax
from jax.experimental import pallas as pl
from jax.experimental.pallas import tpu as pltpu
from jax.sharding import PartitionSpec as P

F32 = jnp.float32
BF16 = jnp.bfloat16
VMEM = pl.BlockSpec(memory_space=pltpu.VMEM)
SMEM = pl.BlockSpec(memory_space=pltpu.SMEM)
ORDER = (0, 1, 3, 2)


def swap_x(value, j):
    return lax.ppermute(value, "col", [(i, i ^ j) for i in range(16)])


def swap_y(value, j):
    return lax.ppermute(value, "col", [(i, i ^ (4 * j)) for i in range(16)])


def swap_row(value, j):
    return lax.ppermute(value, "row", [(i, i ^ j) for i in range(4)])


def encode(value):
    largest = jnp.max(jnp.max(jnp.abs(value), axis=1, keepdims=True), axis=0, keepdims=True)
    power = jnp.clip(jnp.ceil(jnp.log2(jnp.maximum(largest, 1e-30))), -100.0, 100.0)
    scaled = jnp.abs(value) * jnp.exp2(7.5 - power)
    for _ in range(4):
        scaled = scaled * scaled
    rows = jnp.broadcast_to(power, (16, value.shape[1]))
    return jnp.where(value < 0, -scaled, scaled).astype(BF16), rows.astype(BF16)


def decode(ref, start, size):
    tail = ref.shape[0] - 16
    power = ref[tail:, :].astype(F32)[:1, :1]
    code = ref[pl.ds(start, size), :].astype(F32)
    root = jnp.abs(code)
    for _ in range(4):
        root = jnp.sqrt(root)
    root = root * jnp.exp2(power - 7.5)
    return jnp.where(code < 0, -root, root)


def put(ref, value):
    coded, power = encode(value)
    ref[: value.shape[0], :] = coded
    ref[value.shape[0] :, :] = power


def spread(depth, chunks, block, into, place):
    parity = jnp.bitwise_and(depth, 1)
    for ref, own, lead in zip(chunks, (1, 0, 0), (0, 0, 4)):
        for k in range(ref.shape[0] // block):
            source = 2 * (lead + k) + (parity if own else 1 - parity)
            at = pl.multiple_of(place(source) * block, block)
            into[pl.ds(at, block), :] = ref[pl.ds(k * block, block), :]


def grad_inputs_kernel(place_ref, own, near, far, weight_ref, sent, kept, rows):
    block = own.shape[0] // 8

    def place(source):
        j = jnp.bitwise_xor(source, place_ref[1])
        jx, jy = jnp.bitwise_and(j, 3), jnp.right_shift(j, 2)
        slot = jnp.where(jx == 0, 2, jnp.where(jx == 3, 3, jx - 1))
        return slot * 4 + jnp.bitwise_xor(jy, jnp.right_shift(jy, 1))

    spread(place_ref[0], (own, near, far), block, rows, place)
    half = 8 * block
    for at, ref in ((0, sent), (half, kept)):
        part = lax.dot_general(
            rows[pl.ds(at, half), :],
            weight_ref[...],
            (((1,), (1,)), ((), ())),
            preferred_element_type=F32,
        )
        if at:
            ref[...] = part
        else:
            put(ref, part)


def x_stage_kernel(mine, got, sent, kept):
    size = mine.shape[0] // 2
    put(sent, mine[size:, :] + decode(got, size, size))
    kept[...] = mine[:size, :] + decode(got, 0, size)


def y_stage_kernel(mine, got, sent, kept):
    block = mine.shape[0] // 4
    total = mine[...] + decode(got, 0, mine.shape[0])
    put(sent, jnp.concatenate([total[block : 2 * block], total[3 * block :]]))
    kept[:block, :] = total[:block]
    kept[block:, :] = total[2 * block : 3 * block]


def last_stage_kernel(mine, got, sent, kept):
    block = mine.shape[0] // 2
    kept[...] = mine[:block, :] + decode(got, 0, block)
    sent[...] = mine[block:, :] + decode(got, block, block)


def finish_weight_kernel(mine, got, out):
    out[...] = (mine[...] + decode(got, 0, mine.shape[0])).astype(BF16)


def stage(kernel, sent, kept, *operands):
    return pl.pallas_call(
        kernel,
        out_shape=[sent, kept],
        in_specs=[VMEM] * len(operands),
        out_specs=[VMEM] * 2,
        compiler_params=pltpu.CompilerParams(vmem_limit_bytes=10 << 20),
    )(*operands)


def grad_weight_kernel(row_ref, _, grads, near, far, sent, kept, tokens, total):
    quarter = near.shape[0] // 2
    for slot, (ref, at) in enumerate(((near, quarter), (far, quarter), (near, 0), (far, 0))):
        tokens[pl.ds(slot * quarter, quarter), :] = ref[pl.ds(at, quarter), :]
    total[...] = lax.dot_general(
        tokens[...], grads[...], (((0,), (0,)), ((), ())), preferred_element_type=F32
    )
    rows = total.shape[0] // 4
    for jy in range(2):
        for jc, ref in ((1, sent), (0, kept)):
            source = jnp.bitwise_xor(row_ref[0], jy * 2 + jc) * rows
            ref[pl.ds((1 - jy) * rows, rows), :] = total[pl.ds(pl.multiple_of(source, rows), rows), :]


def sum_weight_kernel(mine, got, sent, kept):
    rows = kept.shape[0]
    put(sent, mine[:rows, :] + got[:rows, :])
    kept[...] = mine[rows:, :] + got[rows:, :]


def per_device(inputs, weight, grad_out):
    block, width = inputs.shape
    columns = weight.shape[1]
    tokens = block * 16
    depth, col, row = (lax.axis_index(a) for a in ("depth", "col", "row"))
    ring = [inputs] + [swap_y(inputs, j) for j in ORDER[1:]]
    own = lax.all_gather(
        grad_out,
        "depth",
        axis=0,
        tiled=True,
        axis_index_groups=[list(range(parity, 16, 2)) for parity in range(2)],
    )
    near = lax.ppermute(own[: tokens // 4], "depth", [(i, i ^ 1) for i in range(16)])
    far = lax.ppermute(own[tokens // 4 :], "depth", [(i, ((i + 1) ^ 1) - 1 & 15) for i in range(16)])
    grads = (own, near, far)
    along_y = jnp.concatenate(ring)
    near_in = jnp.concatenate([along_y, swap_x(along_y, 1)])
    far_in = swap_x(near_in, 3)

    def plain(rows, cols=width):
        return jax.ShapeDtypeStruct((rows, cols), F32)

    def coded(rows, cols=width):
        return jax.ShapeDtypeStruct((rows + 16, cols), BF16)

    sent, kept, ordered = pl.pallas_call(
        grad_inputs_kernel,
        out_shape=[coded(tokens // 2), plain(tokens // 2), jax.ShapeDtypeStruct((tokens, columns), BF16)],
        in_specs=[SMEM] + [VMEM] * 4,
        out_specs=[VMEM] * 3,
        compiler_params=pltpu.CompilerParams(vmem_limit_bytes=10 << 20),
        cost_estimate=pl.CostEstimate(
            flops=2 * tokens * width * columns, bytes_accessed=6 << 20, transcendentals=0
        ),
        name="grad_inputs",
    )(jnp.stack([depth, col]), *grads, weight)
    got = swap_x(sent, 1)
    sent, kept = stage(x_stage_kernel, coded(tokens // 4), plain(tokens // 4), kept, got)
    got = swap_x(sent, 3)

    send_w, keep_w = pl.pallas_call(
        grad_weight_kernel,
        out_shape=[plain(width // 2, columns)] * 2,
        in_specs=[SMEM, pl.BlockSpec(memory_space=pl.ANY)] + [VMEM] * 3,
        out_specs=[VMEM] * 2,
        scratch_shapes=[pltpu.VMEM((tokens, width), BF16), pltpu.VMEM((width, columns), F32)],
        compiler_params=pltpu.CompilerParams(vmem_limit_bytes=9 << 20),
        cost_estimate=pl.CostEstimate(
            flops=2 * tokens * width * columns, bytes_accessed=7 << 20, transcendentals=0
        ),
        name="grad_weight",
    )(row.reshape(1), got, ordered, near_in, far_in)
    rows = width // 4
    got_w = swap_row(send_w, 1)
    sent_w, kept_w = stage(sum_weight_kernel, coded(rows, columns), plain(rows, columns), keep_w, got_w)
    got_w = swap_row(sent_w, 2)

    sent, kept = stage(y_stage_kernel, coded(tokens // 8), plain(tokens // 8), kept, got)
    got = swap_y(sent, 1)
    sent, kept = stage(last_stage_kernel, plain(block), plain(block), kept, got)
    grad_inputs = (kept + swap_y(sent, 3)).astype(BF16)
    grad_weight = pl.pallas_call(
        finish_weight_kernel,
        out_shape=jax.ShapeDtypeStruct((rows, columns), BF16),
        in_specs=[VMEM] * 2,
        out_specs=VMEM,
        compiler_params=pltpu.CompilerParams(vmem_limit_bytes=10 << 20),
    )(kept_w, got_w)
    return grad_inputs, grad_weight


def solution(mesh):
    placed = (P(("row", "col"), "depth"), P("depth", "col"), P(("row", "depth"), "col"))
    return jax.shard_map(
        per_device,
        mesh=mesh,
        in_specs=placed,
        out_specs=(P(("row", "col"), "depth"), P(("depth", "row"), "col")),
        check_vma=False,
    )
```

```python
import jax
import jax.numpy as jnp
from jax import lax
from jax.experimental import pallas as pl
from jax.experimental.pallas import tpu as pltpu
from jax.sharding import PartitionSpec as P

F32 = jnp.float32
BF16 = jnp.bfloat16
VMEM = pl.BlockSpec(memory_space=pltpu.VMEM)
SMEM = pl.BlockSpec(memory_space=pltpu.SMEM)
ORDER = (0, 1, 3, 2)


def swap_x(value, j):
    return lax.ppermute(value, "col", [(i, i ^ j) for i in range(16)])


def swap_y(value, j):
    return lax.ppermute(value, "col", [(i, i ^ (4 * j)) for i in range(16)])


def swap_row(value, j):
    return lax.ppermute(value, "row", [(i, i ^ j) for i in range(4)])


def encode(value):
    largest = jnp.max(jnp.max(jnp.abs(value), axis=1, keepdims=True), axis=0, keepdims=True)
    power = jnp.clip(jnp.ceil(jnp.log2(jnp.maximum(largest, 1e-30))), -100.0, 100.0)
    scaled = jnp.abs(value) * jnp.exp2(7.5 - power)
    for _ in range(4):
        scaled = scaled * scaled
    rows = jnp.broadcast_to(power, (16, value.shape[1]))
    return jnp.where(value < 0, -scaled, scaled).astype(BF16), rows.astype(BF16)


def decode(ref, start, size):
    tail = ref.shape[0] - 16
    power = ref[tail:, :].astype(F32)[:1, :1]
    code = ref[pl.ds(start, size), :].astype(F32)
    root = jnp.abs(code)
    for _ in range(4):
        root = jnp.sqrt(root)
    root = root * jnp.exp2(power - 7.5)
    return jnp.where(code < 0, -root, root)


def put(ref, value):
    coded, power = encode(value)
    ref[: value.shape[0], :] = coded
    ref[value.shape[0] :, :] = power


def spread(depth, core, chunks, block, into, place):
    parity = jnp.bitwise_and(depth, 1)
    for ref, own, lead in zip(chunks, (1, 0, 0), (0, 0, 4)):
        for k in range(ref.shape[0] // block):
            rank = jnp.bitwise_xor(lead + k, 7 * core)
            source = 2 * rank + (parity if own else 1 - parity)
            at = pl.multiple_of(place(source) * block, block)
            into[pl.ds(at, block), :] = ref[pl.ds(k * block, block), :]


def grad_inputs_kernel(place_ref, own, near, far, weight_ref, sent, kept, rows):
    block = own.shape[0] // 8

    def place(source):
        j = jnp.bitwise_xor(source, place_ref[1])
        jx, jy = jnp.bitwise_and(j, 3), jnp.right_shift(j, 2)
        slot = jnp.where(jx == 0, 2, jnp.where(jx == 3, 3, jx - 1))
        return slot * 4 + jnp.bitwise_xor(jy, jnp.right_shift(jy, 1))

    spread(place_ref[0], jnp.bitwise_and(place_ref[2], 1), (own, near, far), block, rows, place)
    half = 8 * block
    for at, ref in ((0, sent), (half, kept)):
        part = lax.dot_general(
            rows[pl.ds(at, half), :],
            weight_ref[...],
            (((1,), (1,)), ((), ())),
            preferred_element_type=F32,
        )
        if at:
            ref[...] = part
        else:
            put(ref, part)


def x_stage_kernel(mine, got, sent, kept):
    size = mine.shape[0] // 2
    put(sent, mine[size:, :] + decode(got, size, size))
    kept[...] = mine[:size, :] + decode(got, 0, size)


def y_stage_kernel(mine, got, sent, kept):
    block = mine.shape[0] // 4
    total = mine[...] + decode(got, 0, mine.shape[0])
    put(sent, jnp.concatenate([total[block : 2 * block], total[3 * block :]]))
    kept[:block, :] = total[:block]
    kept[block:, :] = total[2 * block : 3 * block]


def last_stage_kernel(mine, got, sent, kept):
    block = mine.shape[0] // 2
    kept[...] = mine[:block, :] + decode(got, 0, block)
    sent[...] = mine[block:, :] + decode(got, block, block)


def finish_weight_kernel(mine, got, out):
    out[...] = (mine[...] + decode(got, 0, mine.shape[0])).astype(BF16)


def stage(kernel, sent, kept, *operands):
    return pl.pallas_call(
        kernel,
        out_shape=[sent, kept],
        in_specs=[VMEM] * len(operands),
        out_specs=[VMEM] * 2,
        compiler_params=pltpu.CompilerParams(vmem_limit_bytes=10 << 20),
    )(*operands)


def grad_weight_kernel(row_ref, _, grads, near, far, sent, kept, tokens, total):
    quarter = near.shape[0] // 2
    for slot, (ref, at) in enumerate(((near, quarter), (far, quarter), (near, 0), (far, 0))):
        tokens[pl.ds(slot * quarter, quarter), :] = ref[pl.ds(at, quarter), :]
    total[...] = lax.dot_general(
        tokens[...], grads[...], (((0,), (0,)), ((), ())), preferred_element_type=F32
    )
    rows = total.shape[0] // 4
    for jy in range(2):
        for jc, ref in ((1, sent), (0, kept)):
            source = jnp.bitwise_xor(row_ref[0], jy * 2 + jc) * rows
            ref[pl.ds((1 - jy) * rows, rows), :] = total[pl.ds(pl.multiple_of(source, rows), rows), :]


def sum_weight_kernel(mine, got, sent, kept):
    rows = kept.shape[0]
    put(sent, mine[:rows, :] + got[:rows, :])
    kept[...] = mine[rows:, :] + got[rows:, :]


def per_device(inputs, weight, grad_out):
    block, width = inputs.shape
    columns = weight.shape[1]
    tokens = block * 16
    depth, col, row = (lax.axis_index(a) for a in ("depth", "col", "row"))
    ring = [inputs] + [swap_y(inputs, j) for j in ORDER[1:]]
    own = lax.all_gather(
        grad_out,
        ("row", "depth"),
        axis=0,
        tiled=True,
        axis_index_groups=[
            [r * 16 + z for z in range(parity, 16, 2)][:: 1 - 2 * (r % 2)]
            for r in range(4)
            for parity in range(2)
        ],
    )
    near = lax.ppermute(own[: tokens // 4], "depth", [(i, i ^ 1) for i in range(16)])
    far = lax.ppermute(own[tokens // 4 :], "depth", [(i, ((i + 1) ^ 1) - 1 & 15) for i in range(16)])
    grads = (own, near, far)
    along_y = jnp.concatenate(ring)
    near_in = jnp.concatenate([along_y, swap_x(along_y, 1)])
    far_in = swap_x(near_in, 3)

    def plain(rows, cols=width):
        return jax.ShapeDtypeStruct((rows, cols), F32)

    def coded(rows, cols=width):
        return jax.ShapeDtypeStruct((rows + 16, cols), BF16)

    sent, kept, ordered = pl.pallas_call(
        grad_inputs_kernel,
        out_shape=[coded(tokens // 2), plain(tokens // 2), jax.ShapeDtypeStruct((tokens, columns), BF16)],
        in_specs=[SMEM] + [VMEM] * 4,
        out_specs=[VMEM] * 3,
        compiler_params=pltpu.CompilerParams(vmem_limit_bytes=10 << 20),
        cost_estimate=pl.CostEstimate(
            flops=2 * tokens * width * columns, bytes_accessed=6 << 20, transcendentals=0
        ),
        name="grad_inputs",
    )(jnp.stack([depth, col, row]), *grads, weight)
    got = swap_x(sent, 1)
    sent, kept = stage(x_stage_kernel, coded(tokens // 4), plain(tokens // 4), kept, got)
    got = swap_x(sent, 3)

    send_w, keep_w = pl.pallas_call(
        grad_weight_kernel,
        out_shape=[plain(width // 2, columns)] * 2,
        in_specs=[SMEM, pl.BlockSpec(memory_space=pl.ANY)] + [VMEM] * 3,
        out_specs=[VMEM] * 2,
        scratch_shapes=[pltpu.VMEM((tokens, width), BF16), pltpu.VMEM((width, columns), F32)],
        compiler_params=pltpu.CompilerParams(vmem_limit_bytes=9 << 20),
        cost_estimate=pl.CostEstimate(
            flops=2 * tokens * width * columns, bytes_accessed=7 << 20, transcendentals=0
        ),
        name="grad_weight",
    )(row.reshape(1), got, ordered, near_in, far_in)
    rows = width // 4
    got_w = swap_row(send_w, 1)
    sent_w, kept_w = stage(sum_weight_kernel, coded(rows, columns), plain(rows, columns), keep_w, got_w)
    got_w = swap_row(sent_w, 2)

    sent, kept = stage(y_stage_kernel, coded(tokens // 8), plain(tokens // 8), kept, got)
    got = swap_y(sent, 1)
    sent, kept = stage(last_stage_kernel, plain(block), plain(block), kept, got)
    grad_inputs = (kept + swap_y(sent, 3)).astype(BF16)
    grad_weight = pl.pallas_call(
        finish_weight_kernel,
        out_shape=jax.ShapeDtypeStruct((rows, columns), BF16),
        in_specs=[VMEM] * 2,
        out_specs=VMEM,
        compiler_params=pltpu.CompilerParams(vmem_limit_bytes=10 << 20),
    )(kept_w, got_w)
    return grad_inputs, grad_weight


def solution(mesh):
    placed = (P(("row", "col"), "depth"), P("depth", "col"), P(("row", "depth"), "col"))
    return jax.shard_map(
        per_device,
        mesh=mesh,
        in_specs=placed,
        out_specs=(P(("row", "col"), "depth"), P(("depth", "row"), "col")),
        check_vma=False,
    )
```

```python
import jax
import jax.numpy as jnp
from jax import lax
from jax.experimental import pallas as pl
from jax.experimental.pallas import tpu as pltpu
from jax.sharding import PartitionSpec as P

F32 = jnp.float32
BF16 = jnp.bfloat16
VMEM = pl.BlockSpec(memory_space=pltpu.VMEM)
SMEM = pl.BlockSpec(memory_space=pltpu.SMEM)
ORDER = (0, 1, 3, 2)


def swap_x(value, j):
    return lax.ppermute(value, "col", [(i, i ^ j) for i in range(16)])


def swap_y(value, j):
    return lax.ppermute(value, "col", [(i, i ^ (4 * j)) for i in range(16)])


def swap_row(value, j):
    return lax.ppermute(value, "row", [(i, i ^ j) for i in range(4)])


def encode(value):
    largest = jnp.max(jnp.max(jnp.abs(value), axis=1, keepdims=True), axis=0, keepdims=True)
    power = jnp.clip(jnp.ceil(jnp.log2(jnp.maximum(largest, 1e-30))), -100.0, 100.0)
    scaled = jnp.abs(value) * jnp.exp2(7.5 - power)
    for _ in range(4):
        scaled = scaled * scaled
    rows = jnp.broadcast_to(power, (16, value.shape[1]))
    return jnp.where(value < 0, -scaled, scaled).astype(BF16), rows.astype(BF16)


def decode(ref, start, size):
    tail = ref.shape[0] - 16
    power = ref[tail:, :].astype(F32)[:1, :1]
    code = ref[pl.ds(start, size), :].astype(F32)
    root = jnp.exp2(jnp.log2(jnp.maximum(jnp.abs(code), 1e-37)) * 0.0625 + (power - 7.5))
    return jnp.where(code == 0, 0.0, jnp.where(code < 0, -root, root))


def put(ref, value):
    coded, power = encode(value)
    ref[: value.shape[0], :] = coded
    ref[value.shape[0] :, :] = power


def spread(depth, core, chunks, block, into, place):
    parity = jnp.bitwise_and(depth, 1)
    for ref, own, lead in zip(chunks, (1, 0, 0), (0, 0, 4)):
        for k in range(ref.shape[0] // block):
            rank = jnp.bitwise_xor(lead + k, 7 * core)
            source = 2 * rank + (parity if own else 1 - parity)
            at = pl.multiple_of(place(source) * block, block)
            into[pl.ds(at, block), :] = ref[pl.ds(k * block, block), :]


def grad_inputs_kernel(place_ref, own, near, far, weight_ref, sent, kept, rows):
    block = own.shape[0] // 8

    def place(source):
        j = jnp.bitwise_xor(source, place_ref[1])
        jx, jy = jnp.bitwise_and(j, 3), jnp.right_shift(j, 2)
        slot = jnp.where(jx == 0, 2, jnp.where(jx == 3, 3, jx - 1))
        return slot * 4 + jnp.bitwise_xor(jy, jnp.right_shift(jy, 1))

    spread(place_ref[0], jnp.bitwise_and(place_ref[2], 1), (own, near, far), block, rows, place)
    half = 8 * block
    for at, ref in ((0, sent), (half, kept)):
        part = lax.dot_general(
            rows[pl.ds(at, half), :],
            weight_ref[...],
            (((1,), (1,)), ((), ())),
            preferred_element_type=F32,
        )
        if at:
            ref[...] = part
        else:
            put(ref, part)


def x_stage_kernel(mine, got, sent, kept):
    size = mine.shape[0] // 2
    put(sent, mine[size:, :] + decode(got, size, size))
    kept[...] = mine[:size, :] + decode(got, 0, size)


def y_stage_kernel(mine, got, sent, kept):
    block = mine.shape[0] // 4
    total = mine[...] + decode(got, 0, mine.shape[0])
    put(sent, jnp.concatenate([total[block : 2 * block], total[3 * block :]]))
    kept[:block, :] = total[:block]
    kept[block:, :] = total[2 * block : 3 * block]


def last_stage_kernel(mine, got, sent, kept):
    block = mine.shape[0] // 2
    kept[...] = mine[:block, :] + decode(got, 0, block)
    put(sent, mine[block:, :] + decode(got, block, block))


def finish_kernel(mine, got, out):
    out[...] = (mine[...] + decode(got, 0, mine.shape[0])).astype(BF16)


def finish(kept, got):
    return pl.pallas_call(
        finish_kernel,
        out_shape=jax.ShapeDtypeStruct(kept.shape, BF16),
        in_specs=[VMEM] * 2,
        out_specs=VMEM,
        compiler_params=pltpu.CompilerParams(vmem_limit_bytes=10 << 20),
    )(kept, got)


def stage(kernel, sent, kept, *operands, weight=0):
    return pl.pallas_call(
        kernel,
        out_shape=[sent, kept],
        in_specs=[VMEM] * len(operands),
        out_specs=[VMEM] * 2,
        compiler_params=pltpu.CompilerParams(vmem_limit_bytes=10 << 20),
        cost_estimate=pl.CostEstimate(flops=weight, bytes_accessed=1 << 20, transcendentals=0),
    )(*operands)


def grad_weight_kernel(row_ref, _, grads, near, far, sent, kept, tokens, total):
    quarter = near.shape[0] // 2
    for slot, (ref, at) in enumerate(((near, quarter), (far, quarter), (near, 0), (far, 0))):
        tokens[pl.ds(slot * quarter, quarter), :] = ref[pl.ds(at, quarter), :]
    total[...] = lax.dot_general(
        tokens[...], grads[...], (((0,), (0,)), ((), ())), preferred_element_type=F32
    )
    rows = total.shape[0] // 4
    for jy in range(2):
        for jc, ref in ((1, sent), (0, kept)):
            source = jnp.bitwise_xor(row_ref[0], jy * 2 + jc) * rows
            ref[pl.ds((1 - jy) * rows, rows), :] = total[pl.ds(pl.multiple_of(source, rows), rows), :]


def sum_weight_kernel(mine, got, sent, kept):
    rows = kept.shape[0]
    put(sent, mine[:rows, :] + got[:rows, :])
    kept[...] = mine[rows:, :] + got[rows:, :]


def per_device(inputs, weight, grad_out):
    block, width = inputs.shape
    columns = weight.shape[1]
    tokens = block * 16
    depth, col, row = (lax.axis_index(a) for a in ("depth", "col", "row"))
    ring = [inputs] + [swap_y(inputs, j) for j in ORDER[1:]]
    own = lax.all_gather(
        grad_out,
        ("row", "depth"),
        axis=0,
        tiled=True,
        axis_index_groups=[
            [r * 16 + z for z in range(parity, 16, 2)][:: 1 - 2 * (r % 2)]
            for r in range(4)
            for parity in range(2)
        ],
    )
    near = lax.ppermute(own[: tokens // 4], "depth", [(i, i ^ 1) for i in range(16)])
    far = lax.ppermute(own[tokens // 4 :], "depth", [(i, ((i + 1) ^ 1) - 1 & 15) for i in range(16)])
    grads = (own, near, far)
    along_y = jnp.concatenate(ring)
    near_in = jnp.concatenate([along_y, swap_x(along_y, 1)])
    far_in = swap_x(near_in, 3)

    def plain(rows, cols=width):
        return jax.ShapeDtypeStruct((rows, cols), F32)

    def coded(rows, cols=width):
        return jax.ShapeDtypeStruct((rows + 16, cols), BF16)

    sent, kept, ordered = pl.pallas_call(
        grad_inputs_kernel,
        out_shape=[coded(tokens // 2), plain(tokens // 2), jax.ShapeDtypeStruct((tokens, columns), BF16)],
        in_specs=[SMEM] + [VMEM] * 4,
        out_specs=[VMEM] * 3,
        compiler_params=pltpu.CompilerParams(vmem_limit_bytes=10 << 20),
        cost_estimate=pl.CostEstimate(
            flops=2 * tokens * width * columns, bytes_accessed=6 << 20, transcendentals=0
        ),
        name="grad_inputs",
    )(jnp.stack([depth, col, row]), *grads, weight)
    got = swap_x(sent, 1)
    sent, kept = stage(x_stage_kernel, coded(tokens // 4), plain(tokens // 4), kept, got)
    got = swap_x(sent, 3)

    send_w, keep_w = pl.pallas_call(
        grad_weight_kernel,
        out_shape=[plain(width // 2, columns)] * 2,
        in_specs=[SMEM, pl.BlockSpec(memory_space=pl.ANY)] + [VMEM] * 3,
        out_specs=[VMEM] * 2,
        scratch_shapes=[pltpu.VMEM((tokens, width), BF16), pltpu.VMEM((width, columns), F32)],
        compiler_params=pltpu.CompilerParams(vmem_limit_bytes=9 << 20),
        cost_estimate=pl.CostEstimate(
            flops=2 * tokens * width * columns, bytes_accessed=7 << 20, transcendentals=0
        ),
        name="grad_weight",
    )(row.reshape(1), got, ordered, near_in, far_in)
    rows = width // 4
    got_w = swap_row(send_w, 1)
    sent, kept = stage(y_stage_kernel, coded(tokens // 8), plain(tokens // 8), kept, got)
    sent_w, kept_w = stage(sum_weight_kernel, coded(rows, columns), plain(rows, columns), keep_w, got_w)
    got_w = swap_row(sent_w, 2)
    got = swap_y(sent, 1)
    sent, kept = stage(last_stage_kernel, coded(block), plain(block), kept, got, weight=8 << 30)
    got = swap_y(sent, 3)
    grad_weight = finish(kept_w, got_w)
    return finish(kept, got), grad_weight


def solution(mesh):
    placed = (P(("row", "col"), "depth"), P("depth", "col"), P(("row", "depth"), "col"))
    return jax.shard_map(
        per_device,
        mesh=mesh,
        in_specs=placed,
        out_specs=(P(("row", "col"), "depth"), P(("depth", "row"), "col")),
        check_vma=False,
    )
```

```python
import jax
import jax.numpy as jnp
from jax import lax
from jax.experimental import pallas as pl
from jax.experimental.pallas import tpu as pltpu
from jax.sharding import PartitionSpec as P

F32 = jnp.float32
BF16 = jnp.bfloat16
VMEM = pl.BlockSpec(memory_space=pltpu.VMEM)
SMEM = pl.BlockSpec(memory_space=pltpu.SMEM)
ORDER = (0, 1, 3, 2)


def swap_x(value, j):
    return lax.ppermute(value, "col", [(i, i ^ j) for i in range(16)])


def swap_y(value, j):
    return lax.ppermute(value, "col", [(i, i ^ (4 * j)) for i in range(16)])


def swap_row(value, j):
    return lax.ppermute(value, "row", [(i, i ^ j) for i in range(4)])


def encode(value):
    largest = jnp.max(jnp.max(jnp.abs(value), axis=1, keepdims=True), axis=0, keepdims=True)
    power = jnp.clip(jnp.ceil(jnp.log2(jnp.maximum(largest, 1e-30))), -100.0, 100.0)
    scaled = jnp.abs(value) * jnp.exp2(7.5 - power)
    for _ in range(4):
        scaled = scaled * scaled
    rows = jnp.broadcast_to(power, (16, value.shape[1]))
    return jnp.where(value < 0, -scaled, scaled).astype(BF16), rows.astype(BF16)


def decode(ref, start, size):
    tail = ref.shape[0] - 16
    power = ref[tail:, :].astype(F32)[:1, :1]
    code = ref[pl.ds(start, size), :].astype(F32)
    root = jnp.exp2(jnp.log2(jnp.maximum(jnp.abs(code), 1e-37)) * 0.0625 + (power - 7.5))
    return jnp.where(code == 0, 0.0, jnp.where(code < 0, -root, root))


def put(ref, value):
    coded, power = encode(value)
    ref[: value.shape[0], :] = coded
    ref[value.shape[0] :, :] = power


def spread(depth, core, chunks, block, into, place):
    parity = jnp.bitwise_and(depth, 1)
    for ref, own, lead in zip(chunks, (1, 0, 0), (0, 0, 4)):
        for k in range(ref.shape[0] // block):
            rank = jnp.bitwise_xor(lead + k, 7 * core)
            source = 2 * rank + (parity if own else 1 - parity)
            at = pl.multiple_of(place(source) * block, block)
            into[pl.ds(at, block), :] = ref[pl.ds(k * block, block), :]


def grad_inputs_kernel(place_ref, own, near, far, weight_ref, sent, kept, rows):
    block = own.shape[0] // 8

    def place(source):
        j = jnp.bitwise_xor(source, place_ref[1])
        jx, jy = jnp.bitwise_and(j, 3), jnp.right_shift(j, 2)
        slot = jnp.where(jx == 0, 2, jnp.where(jx == 3, 3, jx - 1))
        return slot * 4 + jnp.bitwise_xor(jy, jnp.right_shift(jy, 1))

    spread(place_ref[0], jnp.bitwise_and(place_ref[2], 1), (own, near, far), block, rows, place)
    half = 8 * block
    for at, ref in ((0, sent), (half, kept)):
        part = lax.dot_general(
            rows[pl.ds(at, half), :],
            weight_ref[...],
            (((1,), (1,)), ((), ())),
            preferred_element_type=F32,
        )
        if at:
            ref[...] = part
        else:
            put(ref, part)


def x_stage_kernel(mine, got, sent, kept):
    size = mine.shape[0] // 2
    put(sent, mine[size:, :] + decode(got, size, size))
    kept[...] = mine[:size, :] + decode(got, 0, size)


def y_stage_kernel(mine, got, sent, kept):
    block = mine.shape[0] // 4
    total = mine[...] + decode(got, 0, mine.shape[0])
    put(sent, jnp.concatenate([total[block : 2 * block], total[3 * block :]]))
    kept[:block, :] = total[:block]
    kept[block:, :] = total[2 * block : 3 * block]


def last_stage_kernel(mine, got, sent, kept):
    block = mine.shape[0] // 2
    kept[...] = mine[:block, :] + decode(got, 0, block)
    put(sent, mine[block:, :] + decode(got, block, block))


def finish_kernel(mine, got, out):
    out[...] = (mine[...] + decode(got, 0, mine.shape[0])).astype(BF16)


def finish(kept, got):
    return pl.pallas_call(
        finish_kernel,
        out_shape=jax.ShapeDtypeStruct(kept.shape, BF16),
        in_specs=[VMEM] * 2,
        out_specs=VMEM,
        compiler_params=pltpu.CompilerParams(vmem_limit_bytes=10 << 20),
    )(kept, got)


def stage(kernel, sent, kept, *operands, weight=0):
    return pl.pallas_call(
        kernel,
        out_shape=[sent, kept],
        in_specs=[VMEM] * len(operands),
        out_specs=[VMEM] * 2,
        compiler_params=pltpu.CompilerParams(vmem_limit_bytes=10 << 20),
        cost_estimate=pl.CostEstimate(flops=weight, bytes_accessed=1 << 20, transcendentals=0),
    )(*operands)


def grad_weight_kernel(row_ref, _, grads, x1, x2, x0, x3, sent, kept, tokens, total):
    quarter = x0.shape[0]
    for slot, ref in enumerate((x1, x2, x0, x3)):
        tokens[pl.ds(slot * quarter, quarter), :] = ref[...]
    total[...] = lax.dot_general(
        tokens[...], grads[...], (((0,), (0,)), ((), ())), preferred_element_type=F32
    )
    rows = total.shape[0] // 4
    for jy in range(2):
        for jc, ref in ((1, sent), (0, kept)):
            source = jnp.bitwise_xor(row_ref[0], jy * 2 + jc) * rows
            ref[pl.ds((1 - jy) * rows, rows), :] = total[pl.ds(pl.multiple_of(source, rows), rows), :]


def sum_weight_kernel(mine, got, sent, kept):
    rows = kept.shape[0]
    put(sent, mine[:rows, :] + got[:rows, :])
    kept[...] = mine[rows:, :] + got[rows:, :]


def per_device(inputs, weight, grad_out):
    block, width = inputs.shape
    columns = weight.shape[1]
    tokens = block * 16
    depth, col, row = (lax.axis_index(a) for a in ("depth", "col", "row"))
    own = lax.all_gather(
        grad_out,
        ("row", "depth"),
        axis=0,
        tiled=True,
        axis_index_groups=[
            [r * 16 + z for z in range(parity, 16, 2)][:: 1 - 2 * (r % 2)]
            for r in range(4)
            for parity in range(2)
        ],
    )
    own, inputs = lax.optimization_barrier((own, inputs))
    near = lax.ppermute(own[: tokens // 4], "depth", [(i, i ^ 1) for i in range(16)])
    far = lax.ppermute(own[tokens // 4 :], "depth", [(i, ((i + 1) ^ 1) - 1 & 15) for i in range(16)])
    grads = (own, near, far)
    ring = [inputs] + [swap_y(inputs, j) for j in ORDER[1:]]
    x0 = jnp.concatenate(ring)
    x1, x3 = swap_x(x0, 1), swap_x(x0, 3)
    x2 = swap_x(x3, 1)

    def plain(rows, cols=width):
        return jax.ShapeDtypeStruct((rows, cols), F32)

    def coded(rows, cols=width):
        return jax.ShapeDtypeStruct((rows + 16, cols), BF16)

    sent, kept, ordered = pl.pallas_call(
        grad_inputs_kernel,
        out_shape=[coded(tokens // 2), plain(tokens // 2), jax.ShapeDtypeStruct((tokens, columns), BF16)],
        in_specs=[SMEM] + [VMEM] * 4,
        out_specs=[VMEM] * 3,
        compiler_params=pltpu.CompilerParams(vmem_limit_bytes=10 << 20),
        cost_estimate=pl.CostEstimate(
            flops=2 * tokens * width * columns, bytes_accessed=6 << 20, transcendentals=0
        ),
        name="grad_inputs",
    )(jnp.stack([depth, col, row]), *grads, weight)
    got = swap_x(sent, 1)
    sent, kept = stage(x_stage_kernel, coded(tokens // 4), plain(tokens // 4), kept, got)
    got = swap_x(sent, 3)

    send_w, keep_w = pl.pallas_call(
        grad_weight_kernel,
        out_shape=[plain(width // 2, columns)] * 2,
        in_specs=[SMEM, pl.BlockSpec(memory_space=pl.ANY)] + [VMEM] * 5,
        out_specs=[VMEM] * 2,
        scratch_shapes=[pltpu.VMEM((tokens, width), BF16), pltpu.VMEM((width, columns), F32)],
        compiler_params=pltpu.CompilerParams(vmem_limit_bytes=9 << 20),
        cost_estimate=pl.CostEstimate(
            flops=2 * tokens * width * columns, bytes_accessed=7 << 20, transcendentals=0
        ),
        name="grad_weight",
    )(row.reshape(1), got, ordered, x1, x2, x0, x3)
    rows = width // 4
    got_w = swap_row(send_w, 1)
    sent, kept = stage(y_stage_kernel, coded(tokens // 8), plain(tokens // 8), kept, got)
    sent_w, kept_w = stage(sum_weight_kernel, coded(rows, columns), plain(rows, columns), keep_w, got_w)
    got_w = swap_row(sent_w, 2)
    got = swap_y(sent, 1)
    sent, kept = stage(last_stage_kernel, coded(block), plain(block), kept, got, weight=16 << 30)
    got = swap_y(sent, 3)
    grad_weight = finish(kept_w, got_w)
    return finish(kept, got), grad_weight


def solution(mesh):
    placed = (P(("row", "col"), "depth"), P("depth", "col"), P(("row", "depth"), "col"))
    return jax.shard_map(
        per_device,
        mesh=mesh,
        in_specs=placed,
        out_specs=(P(("row", "col"), "depth"), P(("depth", "row"), "col")),
        check_vma=False,
    )
```

```python
import jax
import jax.numpy as jnp
from jax import lax
from jax.experimental import pallas as pl
from jax.experimental.pallas import tpu as pltpu
from jax.sharding import PartitionSpec as P

F32 = jnp.float32
BF16 = jnp.bfloat16
VMEM = pl.BlockSpec(memory_space=pltpu.VMEM)
SMEM = pl.BlockSpec(memory_space=pltpu.SMEM)
ORDER = (0, 1, 3, 2)


def swap_x(value, j):
    return lax.ppermute(value, "col", [(i, i ^ j) for i in range(16)])


def swap_y(value, j):
    return lax.ppermute(value, "col", [(i, i ^ (4 * j)) for i in range(16)])


def swap_row(value, j):
    return lax.ppermute(value, "row", [(i, i ^ j) for i in range(4)])


def encode(value):
    largest = jnp.max(jnp.max(jnp.abs(value), axis=1, keepdims=True), axis=0, keepdims=True)
    power = jnp.clip(jnp.ceil(jnp.log2(jnp.maximum(largest, 1e-30))), -100.0, 100.0)
    scaled = jnp.abs(value) * jnp.exp2(7.5 - power)
    for _ in range(4):
        scaled = scaled * scaled
    rows = jnp.broadcast_to(power, (16, value.shape[1]))
    return jnp.where(value < 0, -scaled, scaled).astype(BF16), rows.astype(BF16)


def decode(ref, start, size):
    tail = ref.shape[0] - 16
    power = ref[tail:, :].astype(F32)[:1, :1]
    code = ref[pl.ds(start, size), :].astype(F32)
    root = jnp.exp2(jnp.log2(jnp.maximum(jnp.abs(code), 1e-37)) * 0.0625 + (power - 7.5))
    return jnp.where(code == 0, 0.0, jnp.where(code < 0, -root, root))


def put(ref, value):
    coded, power = encode(value)
    ref[: value.shape[0], :] = coded
    ref[value.shape[0] :, :] = power


def spread(depth, core, chunks, block, into, place):
    parity = jnp.bitwise_and(depth, 1)
    for ref, own, lead in zip(chunks, (1, 0, 0), (0, 0, 4)):
        for k in range(ref.shape[0] // block):
            rank = jnp.bitwise_xor(lead + k, 7 * core)
            source = 2 * rank + (parity if own else 1 - parity)
            at = pl.multiple_of(place(source) * block, block)
            into[pl.ds(at, block), :] = ref[pl.ds(k * block, block), :]


def grad_inputs_kernel(place_ref, own, near, far, weight_ref, sent, kept, rows):
    block = own.shape[0] // 8

    def place(source):
        j = jnp.bitwise_xor(source, place_ref[1])
        jx, jy = jnp.bitwise_and(j, 3), jnp.right_shift(j, 2)
        slot = jnp.where(jx == 0, 2, jnp.where(jx == 3, 3, jx - 1))
        return slot * 4 + jnp.bitwise_xor(jy, jnp.right_shift(jy, 1))

    spread(place_ref[0], jnp.bitwise_and(place_ref[2], 1), (own, near, far), block, rows, place)
    half = 8 * block
    for at, ref in ((0, sent), (half, kept)):
        part = lax.dot_general(
            rows[pl.ds(at, half), :],
            weight_ref[...],
            (((1,), (1,)), ((), ())),
            preferred_element_type=F32,
        )
        if at:
            ref[...] = part
        else:
            put(ref, part)


def x_stage_kernel(mine, got, sent, kept):
    size = mine.shape[0] // 2
    put(sent, mine[size:, :] + decode(got, size, size))
    kept[...] = mine[:size, :] + decode(got, 0, size)


def y_stage_kernel(mine, got, sent, kept):
    block = mine.shape[0] // 4
    total = mine[...] + decode(got, 0, mine.shape[0])
    put(sent, jnp.concatenate([total[block : 2 * block], total[3 * block :]]))
    kept[:block, :] = total[:block]
    kept[block:, :] = total[2 * block : 3 * block]


def last_stage_kernel(mine, got, sent, kept):
    block = mine.shape[0] // 2
    kept[...] = mine[:block, :] + decode(got, 0, block)
    put(sent, mine[block:, :] + decode(got, block, block))


def finish_kernel(mine, got, out):
    out[...] = (mine[...] + decode(got, 0, mine.shape[0])).astype(BF16)


def finish(kept, got):
    return pl.pallas_call(
        finish_kernel,
        out_shape=jax.ShapeDtypeStruct(kept.shape, BF16),
        in_specs=[VMEM] * 2,
        out_specs=VMEM,
        compiler_params=pltpu.CompilerParams(vmem_limit_bytes=10 << 20),
    )(kept, got)


def stage(kernel, sent, kept, *operands, weight=0):
    return pl.pallas_call(
        kernel,
        out_shape=[sent, kept],
        in_specs=[VMEM] * len(operands),
        out_specs=[VMEM] * 2,
        compiler_params=pltpu.CompilerParams(vmem_limit_bytes=10 << 20),
        cost_estimate=pl.CostEstimate(flops=weight, bytes_accessed=1 << 20, transcendentals=0),
    )(*operands)


def grad_weight_kernel(row_ref, _, grads, x1, x2, x0, x3, sent, kept, tokens, total):
    quarter = x0.shape[0]
    for slot, ref in enumerate((x1, x2, x0, x3)):
        tokens[pl.ds(slot * quarter, quarter), :] = ref[...]
    total[...] = lax.dot_general(
        tokens[...], grads[...], (((0,), (0,)), ((), ())), preferred_element_type=F32
    )
    rows = total.shape[0] // 4
    for jy in range(2):
        for jc, ref in ((1, sent), (0, kept)):
            source = jnp.bitwise_xor(row_ref[0], jy * 2 + jc) * rows
            ref[pl.ds((1 - jy) * rows, rows), :] = total[pl.ds(pl.multiple_of(source, rows), rows), :]


def sum_weight_kernel(mine, got, sent, kept):
    rows = kept.shape[0]
    put(sent, mine[:rows, :] + got[:rows, :])
    kept[...] = mine[rows:, :] + got[rows:, :]


def per_device(inputs, weight, grad_out):
    block, width = inputs.shape
    columns = weight.shape[1]
    tokens = block * 16
    depth, col, row = (lax.axis_index(a) for a in ("depth", "col", "row"))
    own = lax.all_gather(
        grad_out,
        ("row", "depth"),
        axis=0,
        tiled=True,
        axis_index_groups=[
            [r * 16 + z for z in range(parity, 16, 2)][:: 1 - 2 * (r % 2)]
            for r in range(4)
            for parity in range(2)
        ],
    )
    own, inputs = lax.optimization_barrier((own, inputs))
    near = lax.ppermute(own[: tokens // 4], "depth", [(i, i ^ 1) for i in range(16)])
    far = lax.ppermute(own[tokens // 4 :], "depth", [(i, ((i + 1) ^ 1) - 1 & 15) for i in range(16)])
    grads = (own, near, far)
    ring = [inputs] + [swap_y(inputs, j) for j in ORDER[1:]]
    x0 = jnp.concatenate(ring)
    x1, x3 = swap_x(x0, 1), swap_x(x0, 3)
    x2 = swap_x(x3, 1)

    def plain(rows, cols=width):
        return jax.ShapeDtypeStruct((rows, cols), F32)

    def coded(rows, cols=width):
        return jax.ShapeDtypeStruct((rows + 16, cols), BF16)

    sent, kept, ordered = pl.pallas_call(
        grad_inputs_kernel,
        out_shape=[coded(tokens // 2), plain(tokens // 2), jax.ShapeDtypeStruct((tokens, columns), BF16)],
        in_specs=[SMEM] + [VMEM] * 4,
        out_specs=[VMEM] * 3,
        compiler_params=pltpu.CompilerParams(vmem_limit_bytes=10 << 20),
        cost_estimate=pl.CostEstimate(
            flops=2 * tokens * width * columns, bytes_accessed=6 << 20, transcendentals=0
        ),
        name="grad_inputs",
    )(jnp.stack([depth, col, row]), *grads, weight)
    got = swap_x(sent, 1)
    sent, kept = stage(x_stage_kernel, coded(tokens // 4), plain(tokens // 4), kept, got)
    got = swap_x(sent, 3)

    sent, kept = stage(y_stage_kernel, coded(tokens // 8), plain(tokens // 8), kept, got)
    got = swap_y(sent, 1)
    send_w, keep_w = pl.pallas_call(
        grad_weight_kernel,
        out_shape=[plain(width // 2, columns)] * 2,
        in_specs=[SMEM, pl.BlockSpec(memory_space=pl.ANY)] + [VMEM] * 5,
        out_specs=[VMEM] * 2,
        scratch_shapes=[pltpu.VMEM((tokens, width), BF16), pltpu.VMEM((width, columns), F32)],
        compiler_params=pltpu.CompilerParams(vmem_limit_bytes=9 << 20),
        cost_estimate=pl.CostEstimate(
            flops=2 * tokens * width * columns, bytes_accessed=7 << 20, transcendentals=0
        ),
        name="grad_weight",
    )(row.reshape(1), got, ordered, x1, x2, x0, x3)
    rows = width // 4
    got_w = swap_row(send_w, 1)
    sent_w, kept_w = stage(sum_weight_kernel, coded(rows, columns), plain(rows, columns), keep_w, got_w)
    got_w = swap_row(sent_w, 2)
    sent, kept = stage(last_stage_kernel, coded(block), plain(block), kept, got, weight=16 << 30)
    got = swap_y(sent, 3)
    grad_weight = finish(kept_w, got_w)
    return finish(kept, got), grad_weight


def solution(mesh):
    placed = (P(("row", "col"), "depth"), P("depth", "col"), P(("row", "depth"), "col"))
    return jax.shard_map(
        per_device,
        mesh=mesh,
        in_specs=placed,
        out_specs=(P(("row", "col"), "depth"), P(("depth", "row"), "col")),
        check_vma=False,
    )
```
